256 devices in a mesh: tile: 64 (over x, z, y_lo), layer: 4 (over y_hi, core).
Axes of the slice: x: 4, y: 4 (y_hi: 2, y_lo: 2; y = y_hi * 2 + y_lo), z: 8, core: 2. Of those that a mesh axis runs over, the one named last changes fastest.
Arguments:
- velocity: float32 [2, 1024, 3072], P(None, 'tile'), may hold values from -6 to 6
- friction: float32 [1024, 3072], P('tile'), may hold values from -1 to 1
- thickness: float32 [1024, 3072], P('tile'), may hold values from 0.5 to 2
- rate: float32 [16, 1024, 3072], P('layer', 'tile'), may hold values from 0.5 to 2
- driving: float32 [2, 1024, 3072], P(None, 'tile'), may hold values from -6 to 6
- ice_mask: int32 [1024, 3072], P('tile'), may hold values from 0 to 2
- obs_velocity: float32 [64, 4, 64, 256], P('tile', 'layer'), may hold values from -6 to 6
- obs_weight: float32 [64, 4, 64, 128], P('tile', 'layer'), may hold values from 0.2 to 1
- obs_cells: int32 [64, 4, 64, 128], P('tile', 'layer'), may hold values from 0 to 49151
- obs_counts: int32 [64, 4, 64], P('tile', 'layer'), may hold values from 0 to 128, as said below
Outputs:
- friction_out: float32 [1024, 3072], P('tile')
- velocity_out: float32 [2, 1024, 3072], P(None, 'tile')
The draws below stay inside these ranges and needn't reach their ends.
Inputs may be any that keep to these rules, and one draw needn't show every extreme that they name: `obs_counts`: in every draw one owner strip receives 128 live slots from every source share.
All inputs are finite; a program needn't handle non-finite values.
Results may differ from the reference program's by a relative error of at most 0.00002.
Values sent between devices are 32-bit elements; how exact they have to be, the bound alone decides.
A program may use at most 128 MiB of HBM per device.

```python
import math
import jax
import jax.numpy as jnp

CX = 16
NY = 3072
CAP = 128
ITERS = 2
LAYERS = 16
NX = 1024
N_TILE = 64
N_LAYER = 4


def draw_obs_counts(key, part):
    key = jax.random.fold_in(key, 7)
    first, second = jax.random.split(key)
    counts = jax.random.randint(first, (N_TILE, N_LAYER, N_TILE), 0, CAP + 1)
    hottest = jax.random.randint(second, (), 0, N_TILE)
    column = jnp.arange(N_TILE)[None, None, :] == hottest
    return jnp.where(column, CAP, counts).astype(jnp.int32)


def touch_ends(drawn, rng, least, high):
    spot = [jax.random.randint(jax.random.fold_in(rng, axis), (), 0, length) for axis, length in enumerate(drawn.shape)]
    longest = drawn.shape.index(max(drawn.shape))
    neighbour = spot[:longest] + [(spot[longest] + 1) % drawn.shape[longest]] + spot[longest + 1:]
    return drawn.at[tuple(spot)].set(least).at[tuple(neighbour)].set(high)


def steps_of(key, dims, pieces, least, top_value):
    def one(dim, parts):
        heights = jax.random.uniform(jax.random.fold_in(jax.random.fold_in(key, 6), dim), (parts,), jnp.float32, least / len(pieces), top_value / len(pieces))
        return jnp.repeat(jnp.exp(heights), dims[dim] // parts).reshape((-1,) + (1,) * (len(dims) - dim - 1))

    level = one(*pieces[0])
    for cut in pieces[1:]:
        level = level * one(*cut)
    return level


def noise(key, shape, scale, reach, cuts=(), held_as=jnp.bfloat16):
    entries = jax.random.normal(key, shape, jnp.float32) * scale
    if len(cuts) > 0:
        entries = steps_of(key, shape, cuts, -0.22, 0.18) * entries
    return jnp.clip(entries, min=-reach, max=reach).astype(held_as)


def setup_inputs(seed: int = 0) -> dict:
    seeds = jax.random.split(jax.random.key(seed), 11)
    return {
        "velocity": noise(seeds[0], (2, NX, NY), 1.0, 6.0, ((1, 64),), jnp.float32),
        "friction": jnp.clip(jax.random.uniform(seeds[1], (NX, NY), jnp.float32, -1.0, 1.0) * steps_of(seeds[1], (NX, NY), ((0, 64),), -0.4, 0.0), -1.0, 1.0),
        "thickness": jnp.clip(jnp.exp(math.log(2.0) - 1.3862944 * jax.random.uniform(seeds[2], (NX, NY), jnp.float32) ** steps_of(seeds[2], (NX, NY), ((0, 64),), -0.2, 0.2)), 0.5, 2.0),
        "rate": jnp.clip(jnp.exp(math.log(2.0) - 1.3862944 * jax.random.uniform(seeds[3], (LAYERS, NX, NY), jnp.float32) ** steps_of(seeds[3], (LAYERS, NX, NY), ((0, 4), (1, 64)), -0.2, 0.2)), 0.5, 2.0),
        "driving": noise(seeds[4], (2, NX, NY), 1.0, 6.0, ((1, 64),), jnp.float32),
        "ice_mask": touch_ends(jax.random.randint(seeds[5], (NX, NY), 0, 3), jax.random.fold_in(seeds[5], 1), 0, 2).astype(jnp.int32),
        "obs_velocity": noise(seeds[6], (N_TILE, N_LAYER, N_TILE, 2 * CAP), 1.0, 6.0, ((0, 64), (1, 4)), jnp.float32),
        "obs_weight": jnp.clip(jnp.exp(math.log(1.0) - 1.609438 * jax.random.uniform(seeds[7], (N_TILE, N_LAYER, N_TILE, CAP), jnp.float32) ** steps_of(seeds[7], (N_TILE, N_LAYER, N_TILE, CAP), ((0, 64), (1, 4)), -0.2, 0.2)), 0.2, 1.0),
        "obs_cells": touch_ends(jax.random.randint(seeds[8], (N_TILE, N_LAYER, N_TILE, CAP), 0, CX * NY), jax.random.fold_in(seeds[8], 1), 0, (CX * NY) - 1).astype(jnp.int32),
        "obs_counts": draw_obs_counts(jax.random.fold_in(seeds[10], 71), 0),
    }


def diff_rows(field):
    padded = jnp.pad(field, ((1, 1), (0, 0)))
    return 0.5 * (padded[2:, :] - padded[:-2, :])


def diff_cols(field):
    padded = jnp.pad(field, ((0, 0), (1, 1)))
    return 0.5 * (padded[:, 2:] - padded[:, :-2])


def reference(velocity, friction, thickness, rate, driving, ice_mask, obs_velocity, obs_weight, obs_cells, obs_counts):
    grounded = (ice_mask == 2).astype(jnp.float32)
    icy = (ice_mask >= 1).astype(jnp.float32)
    owners = jnp.arange(N_TILE, dtype=jnp.int32)[None, None, :, None] * (CX * NY)
    target = (owners + obs_cells).reshape(-1).astype(jnp.int32)
    live = jnp.arange(CAP, dtype=jnp.int32)[None, None, None, :] < obs_counts[..., None]
    weights = jnp.where(live, obs_weight, jnp.float32(0.0)).reshape(-1)
    seen = jnp.stack([obs_velocity[..., :CAP].reshape(-1), obs_velocity[..., CAP:].reshape(-1)])
    speed = velocity
    coeff = friction
    for step in range(ITERS):
        fric = grounded * jnp.exp(coeff)
        exx = diff_rows(speed[0])
        eyy = diff_cols(speed[1])
        exy = 0.5 * (diff_cols(speed[0]) + diff_rows(speed[1]))
        strain = exx * exx + eyy * eyy + exx * eyy + exy * exy + 0.05
        shear = 0.25 * fric * fric * (speed[0] * speed[0] + speed[1] * speed[1])
        total = jnp.zeros_like(strain)
        for layer_k in range(LAYERS):
            depth = 1.0 - (layer_k + 0.5) / LAYERS
            total = total + rate[layer_k] * (strain + depth * depth * shear) ** (-1.0 / 3.0)
        visc = thickness * (total / LAYERS)
        sxx = 2.0 * visc * (2.0 * exx + eyy)
        syy = 2.0 * visc * (2.0 * eyy + exx)
        sxy = 2.0 * visc * exy
        res_a = diff_rows(sxx) + diff_cols(sxy) - fric * speed[0] + driving[0]
        res_b = diff_rows(sxy) + diff_cols(syy) - fric * speed[1] + driving[1]
        scale = 0.5 * icy / (1.0 + fric + 4.0 * visc)
        speed = jnp.stack([speed[0] + scale * res_a, speed[1] + scale * res_b])
        flat = speed.reshape(2, -1)
        misfit = weights[None, :] * (flat[:, target] - seen)
        adjoint = jnp.zeros((2, NX * NY), jnp.float32).at[:, target].add(misfit).reshape(2, NX, NY)
        coeff = coeff - 0.2 * fric * (speed[0] * adjoint[0] + speed[1] * adjoint[1])
    return coeff, speed
```

```python
import functools
import math

import jax
import jax.numpy as jnp
from jax import lax
from jax.experimental import pallas as pl
from jax.experimental.pallas import tpu as pltpu
from jax.sharding import PartitionSpec as P

ITERS = 2
MESH = pl.DeviceIdType.MESH
LANES = 128
PIECES = 3
CHANNELS = 3


def split_pieces(value):
    pieces = []
    for _ in range(PIECES):
        piece = value.astype(jnp.bfloat16).astype(jnp.float32)
        pieces.append(piece)
        value = value - piece
    return pieces


def kernel(
    n_tile,
    n_layer,
    groups,
    velocity,
    friction,
    thickness,
    rate,
    driving,
    ice_mask,
    obs_velocity,
    obs_weight,
    obs_cells,
    obs_counts,
    friction_out,
    velocity_out,
    packed,
    received,
    left_side,
    right_side,
    total,
    fields,
    from_sibling,
    pair_sum,
    from_partner,
    rates,
    vel,
    edge_left,
    edge_right,
    fric_in,
    thick,
    drive,
    mask,
    row_send,
    row_recv,
    col_send,
    col_recv,
    result,
    load_sems,
    obs_send_sem,
    obs_recv_sems,
    rate_send_sems,
    rate_recv_sems,
    row_send_sems,
    row_recv_sems,
    col_send_sems,
    col_recv_sems,
    sum_send_sems,
    sum_recv_sems,
    out_send_sems,
    out_recv_sems,
    own_sems,
):
    t = lax.axis_index("tile")
    l = lax.axis_index("layer")
    rows, width = friction.shape
    quarter = width // n_layer
    depth = rate.shape[0]
    total_layers = depth * n_layer
    slots = obs_weight.shape[-1]
    per_group = n_tile // groups
    marks = rows * n_layer
    core = lax.rem(l, 2)
    pair = l // 2
    sibling = pair * 2 + (1 - core)
    partner = (1 - pair) * 2 + core
    above = lax.rem(t + n_tile - 1, n_tile)
    below = lax.rem(t + 1, n_tile)
    lefter = lax.rem(l + n_layer - 1, n_layer)
    righter = lax.rem(l + 1, n_layer)
    first = pl.multiple_of(l * quarter, LANES)
    columns = pl.ds(first, quarter)

    def remote(src, dst, send_sem, recv_sem, tile, layer):
        return pltpu.make_async_remote_copy(
            src_ref=src,
            dst_ref=dst,
            send_sem=send_sem,
            recv_sem=recv_sem,
            device_id=(tile, layer),
            device_id_type=MESH,
        )

    before = pl.multiple_of(jnp.maximum(first - LANES, 0), LANES)
    after = pl.multiple_of(jnp.minimum(first + quarter, width - LANES), LANES)
    loads = [
        pltpu.make_async_copy(velocity.at[:, :, columns], vel, load_sems.at[0]),
        pltpu.make_async_copy(velocity.at[:, :, pl.ds(before, LANES)], edge_left, load_sems.at[1]),
        pltpu.make_async_copy(velocity.at[:, :, pl.ds(after, LANES)], edge_right, load_sems.at[2]),
        pltpu.make_async_copy(friction.at[:, columns], fric_in, load_sems.at[3]),
        pltpu.make_async_copy(thickness.at[:, columns], thick, load_sems.at[4]),
        pltpu.make_async_copy(driving.at[:, :, columns], drive, load_sems.at[5]),
        pltpu.make_async_copy(ice_mask.at[:, columns], mask, load_sems.at[6]),
        pltpu.make_async_copy(
            rate.at[:, :, columns], rates.at[pl.ds(l * depth, depth)], load_sems.at[7]
        ),
    ]
    for load in loads:
        load.start()

    barrier = pltpu.get_barrier_semaphore()

    def greet(offset, carry):
        pl.semaphore_signal(
            barrier, inc=1, device_id=(lax.rem(t + offset, n_tile), l), device_id_type=MESH
        )
        return carry

    lax.fori_loop(1, n_tile, greet, 0)
    for offset in range(1, n_layer):
        pl.semaphore_signal(
            barrier, inc=1, device_id=(t, lax.rem(l + offset, n_layer)), device_id_type=MESH
        )

    row_id = lax.broadcasted_iota(jnp.int32, (n_tile, n_tile), 0)
    col_id = lax.broadcasted_iota(jnp.int32, (n_tile, n_tile), 1)
    counts = jnp.sum(
        jnp.where(row_id == col_id, obs_counts[...].astype(jnp.float32), 0.0), axis=1, keepdims=True
    )
    place = lax.broadcasted_iota(jnp.int32, (n_tile, slots), 1).astype(jnp.float32)
    weight = jnp.where(place < counts, obs_weight[...], 0.0)
    packed[:, 0, :] = weight
    packed[:, 1, :] = weight * obs_velocity[:, :slots]
    packed[:, 2, :] = weight * obs_velocity[:, slots:]
    packed[:, 3, :] = obs_cells[...].astype(jnp.float32)
    received[0] = packed[t]

    for load in loads[:3]:
        load.wait()
    row_send[0, 0] = vel[:, 0, :]
    row_send[0, 1] = vel[:, rows - 1, :]

    pl.semaphore_wait(barrier, n_tile - 1 + n_layer - 1)

    def swap_rows(phase):
        copies = [
            remote(
                row_send.at[phase, 0],
                row_recv.at[phase, 1],
                row_send_sems.at[phase, 0],
                row_recv_sems.at[phase, 1],
                above,
                l,
            ),
            remote(
                row_send.at[phase, 1],
                row_recv.at[phase, 0],
                row_send_sems.at[phase, 1],
                row_recv_sems.at[phase, 0],
                below,
                l,
            ),
        ]
        for copy in copies:
            copy.start()
        return copies

    def swap_cols(phase):
        copies = [
            remote(
                col_send.at[phase, 0],
                col_recv.at[phase, 1],
                col_send_sems.at[phase, 0],
                col_recv_sems.at[phase, 1],
                t,
                lefter,
            ),
            remote(
                col_send.at[phase, 1],
                col_recv.at[phase, 0],
                col_send_sems.at[phase, 1],
                col_recv_sems.at[phase, 0],
                t,
                righter,
            ),
        ]
        for copy in copies:
            copy.start()
        return copies

    def send_edges(phase, by_row, by_col):
        for k in range(2):
            row_send[phase, 0, k : k + 1, :] = by_row[k][0:1, :]
            row_send[phase, 1, k : k + 1, :] = by_row[k][rows - 1 : rows, :]
            col_send[phase - 1, 0, k] = by_col[k][:, :LANES]
            col_send[phase - 1, 1, k] = by_col[k][:, quarter - LANES :]
        return swap_rows(phase) + swap_cols(phase - 1)

    first_rows = swap_rows(0)

    def send_obs(offset, carry):
        to = lax.rem(t + offset, n_tile)
        remote(
            packed.at[to],
            received.at[offset],
            obs_send_sem,
            obs_recv_sems.at[offset // per_group],
            to,
            l,
        ).start()
        return carry

    lax.fori_loop(1, n_tile, send_obs, 0)

    rate_copies = []
    for offset in (1, 2, 3):
        to = lax.rem(l + offset, n_layer)
        copy = remote(
            rate.at[:, :, pl.ds(pl.multiple_of(to * quarter, LANES), quarter)],
            rates.at[pl.ds(l * depth, depth)],
            rate_send_sems.at[offset - 1],
            rate_recv_sems.at[offset - 1],
            t,
            to,
        )
        copy.start()
        rate_copies.append(copy)

    total[...] = jnp.zeros_like(total)
    mark_id = lax.broadcasted_iota(jnp.int32, (marks, slots), 0).astype(jnp.float32)
    lane_id = lax.broadcasted_iota(jnp.int32, (slots, quarter), 1).astype(jnp.float32)

    def gather_group(group, count, start):
        return pltpu.make_async_copy(
            received.at[pl.ds(start, count)], received.at[pl.ds(start, count)], obs_recv_sems.at[group]
        )

    def add_group(group):
        block = received[pl.ds(group * per_group, per_group)]
        cell = block[:, 3, :]
        mark = jnp.floor((cell + 0.5) * (1.0 / quarter))
        column = cell - mark * quarter
        row = jnp.floor((mark + 0.5) * (1.0 / n_layer))
        mark = (mark - row * n_layer) * rows + row
        column = column.T
        pieces = []
        for channel in range(CHANNELS):
            pieces += split_pieces(block[:, channel, :])
        for b in range(per_group):
            hit = mark[b : b + 1, :] == mark_id
            for p, piece in enumerate(pieces):
                left_side[p * marks : (p + 1) * marks, b * slots : (b + 1) * slots] = jnp.where(
                    hit, piece[b : b + 1, :], 0.0
                ).astype(jnp.bfloat16)
            right_side[b * slots : (b + 1) * slots, :] = jnp.where(
                column[:, b : b + 1] == lane_id, 1.0, 0.0
            ).astype(jnp.bfloat16)
        total[...] += jnp.dot(left_side[...], right_side[...], preferred_element_type=jnp.float32)

    gather_group(0, per_group - 1, 1).wait()
    add_group(0)

    def later_group(group, carry):
        gather_group(group, per_group, group * per_group).wait()
        add_group(group)
        return carry

    lax.fori_loop(1, groups, later_group, 0)

    def collect(q):
        for channel in range(CHANNELS):
            field = None
            for piece in range(PIECES):
                start = pl.multiple_of((channel * PIECES + piece) * marks + q * rows, rows)
                part = total[pl.ds(start, rows), :]
                field = part if field is None else field + part
            fields[q, channel] = field

    sum_copies = []
    for k, chip in enumerate((1 - pair, pair)):
        q = chip * 2 + (1 - core)
        collect(q)
        copy = remote(
            fields.at[q], from_sibling.at[k], sum_send_sems.at[k], sum_recv_sems.at[k], t, sibling
        )
        copy.start()
        sum_copies.append(copy)
    collect(partner)

    for load in loads[3:]:
        load.wait()
    for copy in rate_copies:
        copy.wait()
    for copy in first_rows:
        copy.wait()

    row_of = lax.broadcasted_iota(jnp.int32, (rows, quarter), 0)
    col_of = lax.broadcasted_iota(jnp.int32, (rows, quarter), 1)
    top, bottom = t == 0, t == n_tile - 1
    leftmost, rightmost = l == 0, l == n_layer - 1

    def diff_rows(field, low, high):
        low = jnp.where(top, 0.0, low)
        high = jnp.where(bottom, 0.0, high)
        previous = jnp.where(row_of == 0, low, pltpu.roll(field, 1, 0))
        following = jnp.where(row_of == rows - 1, high, pltpu.roll(field, rows - 1, 0))
        return 0.5 * (following - previous)

    def diff_cols(field, low, high):
        low = jnp.where(leftmost, 0.0, low)
        high = jnp.where(rightmost, 0.0, high)
        previous = jnp.where(col_of == 0, low, pltpu.roll(field, 1, 1))
        following = jnp.where(col_of == quarter - 1, high, pltpu.roll(field, quarter - 1, 1))
        return 0.5 * (following - previous)

    def row_halo(phase, k):
        return row_recv[phase, 0, k : k + 1, :], row_recv[phase, 1, k : k + 1, :]

    def col_halo(phase, k):
        return (
            col_recv[phase - 1, 0, k, :, LANES - 1 : LANES],
            col_recv[phase - 1, 1, k, :, 0:1],
        )

    grounded = jnp.where(mask[...] == 2, 1.0, 0.0)
    icy = jnp.where(mask[...] >= 1, 1.0, 0.0)

    def strains(speed, rows_0, rows_1, cols_0, cols_1):
        exx = diff_rows(speed[0], *rows_0)
        eyy = diff_cols(speed[1], *cols_1)
        exy = 0.5 * (diff_cols(speed[0], *cols_0) + diff_rows(speed[1], *rows_1))
        return exx, eyy, exy

    def viscosity(strain, speed, fric):
        exx, eyy, exy = strain
        e2 = exx * exx + eyy * eyy + exx * eyy + exy * exy + 0.05
        b2 = 0.25 * fric * fric * (speed[0] * speed[0] + speed[1] * speed[1])
        total_visc = jnp.zeros_like(e2)
        for k in range(total_layers):
            height = 1.0 - (k + 0.5) / total_layers
            total_visc = total_visc + rates[k] * jnp.exp(
                jnp.log(e2 + (height * height) * b2) * (-1.0 / 3.0)
            )
        return thick[...] * (total_visc * (1.0 / total_layers))

    def stresses(strain, visc):
        exx, eyy, exy = strain
        return 2.0 * visc * (2.0 * exx + eyy), 2.0 * visc * (2.0 * eyy + exx), 2.0 * visc * exy

    def new_speed(speed, fric, visc, stress, phase):
        sxx, syy, sxy = stress
        div_0 = diff_rows(sxx, *row_halo(phase, 0)) + diff_cols(sxy, *col_halo(phase, 0))
        div_1 = diff_rows(sxy, *row_halo(phase, 1)) + diff_cols(syy, *col_halo(phase, 1))
        scale = 0.5 * icy / (1.0 + fric + 4.0 * visc)
        return (
            speed[0] + scale * (div_0 - fric * speed[0] + drive[0]),
            speed[1] + scale * (div_1 - fric * speed[1] + drive[1]),
        )

    speed = (vel[0], vel[1])
    coeff = fric_in[...]
    fric = grounded * jnp.exp(coeff)
    strain = strains(
        speed,
        row_halo(0, 0),
        row_halo(0, 1),
        (edge_left[0, :, LANES - 1 : LANES], edge_right[0, :, 0:1]),
        (edge_left[1, :, LANES - 1 : LANES], edge_right[1, :, 0:1]),
    )
    visc = viscosity(strain, speed, fric)
    stress = stresses(strain, visc)
    edges = send_edges(1, (stress[0], stress[2]), (stress[2], stress[1]))

    sum_copies[0].wait()
    pair_sum[...] = fields[partner] + from_sibling[0]
    cross = remote(pair_sum, from_partner, sum_send_sems.at[2], sum_recv_sems.at[2], t, partner)
    cross.start()
    collect(l)

    for copy in edges:
        copy.wait()
    speed = new_speed(speed, fric, visc, stress, 1)
    edges = send_edges(2, speed, speed)
    sum_copies[1].wait()
    for channel in range(CHANNELS):
        fields[l, channel] = fields[l, channel] + from_sibling[1, channel]
    for copy in edges:
        copy.wait()
    strain = strains(speed, row_halo(2, 0), row_halo(2, 1), col_halo(2, 0), col_halo(2, 1))
    cross.wait()
    weight_sum, seen_0, seen_1 = (fields[l, k] + from_partner[k] for k in range(CHANNELS))

    def new_coeff(coeff, fric, speed):
        along = speed[0] * (weight_sum * speed[0] - seen_0) + speed[1] * (
            weight_sum * speed[1] - seen_1
        )
        return coeff - 0.2 * fric * along

    coeff = new_coeff(coeff, fric, speed)

    fric = grounded * jnp.exp(coeff)
    visc = viscosity(strain, speed, fric)
    stress = stresses(strain, visc)
    for copy in send_edges(3, (stress[0], stress[2]), (stress[2], stress[1])):
        copy.wait()
    speed = new_speed(speed, fric, visc, stress, 3)
    result[0] = speed[0]
    result[1] = speed[1]
    result[2] = new_coeff(coeff, fric, speed)

    finals = [
        pltpu.make_async_copy(result.at[0:2], velocity_out.at[:, :, columns], own_sems.at[0]),
        pltpu.make_async_copy(result.at[2], friction_out.at[:, columns], own_sems.at[1]),
    ]
    for copy in finals:
        copy.start()
    for offset in (1, 2, 3):
        to = lax.rem(l + offset, n_layer)
        pairs = (
            (result.at[0:2], velocity_out.at[:, :, columns]),
            (result.at[2], friction_out.at[:, columns]),
        )
        for k, (src, dst) in enumerate(pairs):
            copy = remote(
                src, dst, out_send_sems.at[offset - 1, k], out_recv_sems.at[offset - 1, k], t, to
            )
            copy.start()
            finals.append(copy)
    for copy in finals:
        copy.wait()

    pltpu.make_async_copy(
        packed.at[pl.ds(1, n_tile - 1)], packed.at[pl.ds(1, n_tile - 1)], obs_send_sem
    ).wait()


def body(
    velocity,
    friction,
    thickness,
    rate,
    driving,
    ice_mask,
    obs_velocity,
    obs_weight,
    obs_cells,
    obs_counts,
):
    n_tile, n_layer = lax.axis_size("tile"), lax.axis_size("layer")
    rows, width = friction.shape
    quarter = width // n_layer
    slots = obs_weight.shape[-1]
    depth = rate.shape[0]
    groups = 8 if n_tile % 8 == 0 else 2
    marks = rows * n_layer
    chunk = (n_tile // groups) * slots
    anywhere = pl.BlockSpec(memory_space=pl.ANY)
    in_vmem = pl.BlockSpec(memory_space=pltpu.VMEM)
    f32 = jnp.float32
    friction_out, velocity_out = pl.pallas_call(
        functools.partial(kernel, n_tile, n_layer, groups),
        out_shape=(
            jax.ShapeDtypeStruct(friction.shape, f32),
            jax.ShapeDtypeStruct(velocity.shape, f32),
        ),
        in_specs=[anywhere] * 6 + [in_vmem] * 4,
        out_specs=(anywhere, anywhere),
        scratch_shapes=[
            pltpu.VMEM((n_tile, 4, slots), f32),
            pltpu.VMEM((n_tile, 4, slots), f32),
            pltpu.VMEM((CHANNELS * PIECES * marks, chunk), jnp.bfloat16),
            pltpu.VMEM((chunk, quarter), jnp.bfloat16),
            pltpu.VMEM((CHANNELS * PIECES * marks, quarter), f32),
            pltpu.VMEM((n_layer, CHANNELS, rows, quarter), f32),
            pltpu.VMEM((2, CHANNELS, rows, quarter), f32),
            pltpu.VMEM((CHANNELS, rows, quarter), f32),
            pltpu.VMEM((CHANNELS, rows, quarter), f32),
            pltpu.VMEM((depth * n_layer, rows, quarter), f32),
            pltpu.VMEM((2, rows, quarter), f32),
            pltpu.VMEM((2, rows, LANES), f32),
            pltpu.VMEM((2, rows, LANES), f32),
            pltpu.VMEM((rows, quarter), f32),
            pltpu.VMEM((rows, quarter), f32),
            pltpu.VMEM((2, rows, quarter), f32),
            pltpu.VMEM((rows, quarter), jnp.int32),
            pltpu.VMEM((4, 2, 2, quarter), f32),
            pltpu.VMEM((4, 2, 2, quarter), f32),
            pltpu.VMEM((3, 2, 2, rows, LANES), f32),
            pltpu.VMEM((3, 2, 2, rows, LANES), f32),
            pltpu.VMEM((3, rows, quarter), f32),
            pltpu.SemaphoreType.DMA((8,)),
            pltpu.SemaphoreType.DMA,
            pltpu.SemaphoreType.DMA((groups,)),
            pltpu.SemaphoreType.DMA((3,)),
            pltpu.SemaphoreType.DMA((3,)),
            pltpu.SemaphoreType.DMA((4, 2)),
            pltpu.SemaphoreType.DMA((4, 2)),
            pltpu.SemaphoreType.DMA((3, 2)),
            pltpu.SemaphoreType.DMA((3, 2)),
            pltpu.SemaphoreType.DMA((3,)),
            pltpu.SemaphoreType.DMA((3,)),
            pltpu.SemaphoreType.DMA((3, 2)),
            pltpu.SemaphoreType.DMA((3, 2)),
            pltpu.SemaphoreType.DMA((2,)),
        ],
        compiler_params=pltpu.CompilerParams(
            collective_id=0, has_side_effects=True, vmem_limit_bytes=40 * 1024 * 1024
        ),
    )(
        velocity,
        friction,
        thickness,
        rate,
        driving,
        ice_mask,
        obs_velocity.reshape(n_tile, 2 * slots),
        obs_weight.reshape(n_tile, slots),
        obs_cells.reshape(n_tile, slots),
        obs_counts.reshape(1, n_tile),
    )
    return friction_out, velocity_out


def solution(mesh):
    placed = (
        P(None, "tile", None),
        P("tile", None),
        P("tile", None),
        P("layer", "tile", None),
        P(None, "tile", None),
        P("tile", None),
        P("tile", "layer", None, None),
        P("tile", "layer", None, None),
        P("tile", "layer", None, None),
        P("tile", "layer", None),
    )
    return jax.shard_map(
        body,
        mesh=mesh,
        in_specs=placed,
        out_specs=(P("tile", None), P(None, "tile", None)),
        check_vma=False,
    )
```

```python
import functools

import jax
import jax.numpy as jnp
from jax import lax
from jax.experimental import pallas as pl
from jax.experimental.pallas import tpu as pltpu
from jax.sharding import PartitionSpec as P

ITERS = 2
MESH = pl.DeviceIdType.MESH
LANES = 128
PIECES = 3
VMEM_BYTES = 58 * 1024 * 1024

CHANNELS = 3


def split_pieces(value):
    pieces = []
    for _ in range(PIECES):
        piece = value.astype(jnp.bfloat16).astype(jnp.float32)
        pieces.append(piece)
        value = value - piece
    return pieces


def kernel(
    sides,
    n_layer,
    velocity,
    friction,
    thickness,
    rate,
    driving,
    ice_mask,
    obs_velocity,
    obs_weight,
    obs_cells,
    obs_counts,
    friction_out,
    velocity_out,
    packed,
    received,
    left_sides,
    right_sides,
    total,
    fields,
    from_sibling,
    pair_sum,
    from_partner,
    rates,
    vel,
    edge_left,
    edge_right,
    fric_in,
    thick,
    drive,
    mask,
    row_send,
    row_recv,
    col_send,
    col_recv,
    result,
    seen_in,
    weight_in,
    cells_in,
    counts_in,
    load_sems,
    obs_send_sem,
    obs_recv_sems,
    rate_send_sems,
    rate_recv_sems,
    row_send_sems,
    row_recv_sems,
    col_send_sems,
    col_recv_sems,
    sum_send_sems,
    sum_recv_sems,
    out_send_sems,
    out_recv_sems,
    own_sems,
):
    n_x, groups, n_y = sides
    per_group = n_x * n_y
    n_tile = groups * per_group
    t = lax.axis_index("tile")
    l = lax.axis_index("layer")
    rows, width = friction.shape
    quarter = width // n_layer
    depth = rate.shape[0]
    total_layers = depth * n_layer
    slots = obs_weight.shape[-1]
    marks = rows * n_layer
    core = lax.rem(l, 2)
    pair = l // 2
    sibling = pair * 2 + (1 - core)
    partner = (1 - pair) * 2 + core
    above = lax.rem(t + n_tile - 1, n_tile)
    below = lax.rem(t + 1, n_tile)
    lefter = lax.rem(l + n_layer - 1, n_layer)
    righter = lax.rem(l + 1, n_layer)
    first = pl.multiple_of(l * quarter, LANES)
    columns = pl.ds(first, quarter)

    def remote(src, dst, send_sem, recv_sem, tile, layer):
        return pltpu.make_async_remote_copy(
            src_ref=src,
            dst_ref=dst,
            send_sem=send_sem,
            recv_sem=recv_sem,
            device_id=(tile, layer),
            device_id_type=MESH,
        )

    before = pl.multiple_of(jnp.maximum(first - LANES, 0), LANES)
    after = pl.multiple_of(jnp.minimum(first + quarter, width - LANES), LANES)
    loads = [
        pltpu.make_async_copy(velocity.at[:, :, columns], vel, load_sems.at[0]),
        pltpu.make_async_copy(velocity.at[:, :, pl.ds(before, LANES)], edge_left, load_sems.at[1]),
        pltpu.make_async_copy(velocity.at[:, :, pl.ds(after, LANES)], edge_right, load_sems.at[2]),
        pltpu.make_async_copy(friction.at[:, columns], fric_in, load_sems.at[3]),
        pltpu.make_async_copy(thickness.at[:, columns], thick, load_sems.at[4]),
        pltpu.make_async_copy(driving.at[:, :, columns], drive, load_sems.at[5]),
        pltpu.make_async_copy(ice_mask.at[:, columns], mask, load_sems.at[6]),
        pltpu.make_async_copy(
            rate.at[:, :, columns], rates.at[pl.ds(l * depth, depth)], load_sems.at[7]
        ),
        pltpu.make_async_copy(obs_velocity, seen_in, load_sems.at[8]),
        pltpu.make_async_copy(obs_weight, weight_in, load_sems.at[9]),
        pltpu.make_async_copy(obs_cells, cells_in, load_sems.at[10]),
        pltpu.make_async_copy(obs_counts, counts_in, load_sems.at[11]),
    ]
    for load in loads:
        load.start()

    barrier = pltpu.get_barrier_semaphore()

    x, z, y = t // (groups * n_y), lax.rem(t // n_y, groups), lax.rem(t, n_y)

    def peer(turn):
        ring = turn // per_group
        step = lax.rem(ring, 2)
        hop = step * ((ring + 1) // 2) + (1 - step) * (groups - ring // 2)
        to_x = lax.rem(x + lax.rem(turn // n_y, n_x), n_x)
        to_z = lax.rem(z + hop, groups)
        to_y = lax.rem(y + turn, n_y)
        return (to_x * groups + to_z) * n_y + to_y

    def greet(turn, carry):
        pl.semaphore_signal(
            barrier, inc=1, device_id=(peer(n_tile - turn), l), device_id_type=MESH
        )
        return carry

    lax.fori_loop(1, n_tile, greet, 0)
    for offset in range(1, n_layer):
        pl.semaphore_signal(
            barrier, inc=1, device_id=(t, lax.rem(l + offset, n_layer)), device_id_type=MESH
        )

    for load in loads[8:]:
        load.wait()
    row_id = lax.broadcasted_iota(jnp.int32, (n_tile, n_tile), 0)
    col_id = lax.broadcasted_iota(jnp.int32, (n_tile, n_tile), 1)
    counts = jnp.sum(
        jnp.where(row_id == col_id, counts_in[...].astype(jnp.float32), 0.0), axis=1, keepdims=True
    )
    place = lax.broadcasted_iota(jnp.int32, (n_tile, slots), 1).astype(jnp.float32)
    weight = jnp.where(place < counts, weight_in[...], 0.0)
    packed[:, 0, :] = weight
    packed[:, 1, :] = weight * seen_in[:, :slots]
    packed[:, 2, :] = weight * seen_in[:, slots:]
    packed[:, 3, :] = cells_in[...].astype(jnp.float32)

    for load in loads[:3]:
        load.wait()
    row_send[0, 0] = vel[:, 0, :]
    row_send[0, 1] = vel[:, rows - 1, :]

    pl.semaphore_wait(barrier, n_tile - 1 + n_layer - 1)

    def swap_rows(phase):
        copies = [
            remote(
                row_send.at[phase, 0],
                row_recv.at[phase, 1],
                row_send_sems.at[phase, 0],
                row_recv_sems.at[phase, 1],
                above,
                l,
            ),
            remote(
                row_send.at[phase, 1],
                row_recv.at[phase, 0],
                row_send_sems.at[phase, 1],
                row_recv_sems.at[phase, 0],
                below,
                l,
            ),
        ]
        for copy in copies:
            copy.start()
        return copies

    def swap_cols(phase):
        copies = [
            remote(
                col_send.at[phase, 0],
                col_recv.at[phase, 1],
                col_send_sems.at[phase, 0],
                col_recv_sems.at[phase, 1],
                t,
                lefter,
            ),
            remote(
                col_send.at[phase, 1],
                col_recv.at[phase, 0],
                col_send_sems.at[phase, 1],
                col_recv_sems.at[phase, 0],
                t,
                righter,
            ),
        ]
        for copy in copies:
            copy.start()
        return copies

    def send_edges(phase, by_row, by_col):
        for k in range(2):
            row_send[phase, 0, k : k + 1, :] = by_row[k][0:1, :]
            row_send[phase, 1, k : k + 1, :] = by_row[k][rows - 1 : rows, :]
            col_send[phase - 1, 0, k] = by_col[k][:, :LANES]
            col_send[phase - 1, 1, k] = by_col[k][:, quarter - LANES :]
        return swap_rows(phase) + swap_cols(phase - 1)

    first_rows = swap_rows(0)

    own_block = pltpu.make_async_copy(packed.at[t], received.at[0], obs_recv_sems.at[0])
    own_block.start()

    def send_obs(turn, carry):
        to = peer(turn)
        remote(
            packed.at[to],
            received.at[turn],
            obs_send_sem,
            obs_recv_sems.at[turn // per_group],
            to,
            l,
        ).start()
        return carry

    def send_rates():
        copies = []
        for offset in (2, 3, 1):
            to = lax.rem(l + offset, n_layer)
            copy = remote(
                rate.at[:, :, pl.ds(pl.multiple_of(to * quarter, LANES), quarter)],
                rates.at[pl.ds(l * depth, depth)],
                rate_send_sems.at[offset - 1],
                rate_recv_sems.at[offset - 1],
                t,
                to,
            )
            copy.start()
            copies.append(copy)
        return copies

    lax.fori_loop(1, n_tile, send_obs, 0)
    rate_copies = send_rates()

    total[...] = jnp.zeros_like(total)
    mark_id = lax.broadcasted_iota(jnp.int32, (marks, slots), 0).astype(jnp.float32)
    lane_id = lax.broadcasted_iota(jnp.int32, (slots, quarter), 1).astype(jnp.float32)

    def build(group, left_side, right_side):
        start = group * per_group
        pltpu.make_async_copy(
            received.at[pl.ds(start, per_group)],
            received.at[pl.ds(start, per_group)],
            obs_recv_sems.at[group],
        ).wait()
        block = received[pl.ds(group * per_group, per_group)]
        cell = block[:, 3, :]
        mark = jnp.floor((cell + 0.5) * (1.0 / quarter))
        column = cell - mark * quarter
        row = jnp.floor((mark + 0.5) * (1.0 / n_layer))
        mark = (mark - row * n_layer) * rows + row
        column = column.T
        pieces = []
        for channel in range(CHANNELS):
            pieces += split_pieces(block[:, channel, :])
        for b in range(per_group):
            hit = mark[b : b + 1, :] == mark_id
            for p, piece in enumerate(pieces):
                left_side[p * marks : (p + 1) * marks, b * slots : (b + 1) * slots] = jnp.where(
                    hit, piece[b : b + 1, :], 0.0
                ).astype(jnp.bfloat16)
            right_side[b * slots : (b + 1) * slots, :] = jnp.where(
                column[:, b : b + 1] == lane_id, 1.0, 0.0
            ).astype(jnp.bfloat16)

    def multiply(left_side, right_side):
        total[...] += jnp.dot(left_side[...], right_side[...], preferred_element_type=jnp.float32)

    even, odd = (left_sides[0], right_sides[0]), (left_sides[1], right_sides[1])

    def two_groups(pair, carry):
        build(2 * pair + 1, *odd)
        multiply(*even)
        build(2 * pair + 2, *even)
        multiply(*odd)
        return carry

    build(0, *even)
    lax.fori_loop(0, groups // 2 - 1, two_groups, 0)
    for load in loads[3:8]:
        load.wait()
    for copy in rate_copies:
        copy.wait()
    for copy in first_rows:
        copy.wait()

    row_of = lax.broadcasted_iota(jnp.int32, (rows, quarter), 0)
    col_of = lax.broadcasted_iota(jnp.int32, (rows, quarter), 1)
    top, bottom = t == 0, t == n_tile - 1
    leftmost, rightmost = l == 0, l == n_layer - 1

    def diff_rows(field, low, high):
        low = jnp.where(top, 0.0, low)
        high = jnp.where(bottom, 0.0, high)
        previous = jnp.where(row_of == 0, low, pltpu.roll(field, 1, 0))
        following = jnp.where(row_of == rows - 1, high, pltpu.roll(field, rows - 1, 0))
        return 0.5 * (following - previous)

    def diff_cols(field, low, high):
        low = jnp.where(leftmost, 0.0, low)
        high = jnp.where(rightmost, 0.0, high)
        previous = jnp.where(col_of == 0, low, pltpu.roll(field, 1, 1))
        following = jnp.where(col_of == quarter - 1, high, pltpu.roll(field, quarter - 1, 1))
        return 0.5 * (following - previous)

    def row_halo(phase, k):
        return row_recv[phase, 0, k : k + 1, :], row_recv[phase, 1, k : k + 1, :]

    def col_halo(phase, k):
        return (
            col_recv[phase - 1, 0, k, :, LANES - 1 : LANES],
            col_recv[phase - 1, 1, k, :, 0:1],
        )

    grounded = jnp.where(mask[...] == 2, 1.0, 0.0)
    icy = jnp.where(mask[...] >= 1, 1.0, 0.0)

    def strains(speed, rows_0, rows_1, cols_0, cols_1):
        exx = diff_rows(speed[0], *rows_0)
        eyy = diff_cols(speed[1], *cols_1)
        exy = 0.5 * (diff_cols(speed[0], *cols_0) + diff_rows(speed[1], *rows_1))
        return exx, eyy, exy

    def viscosity(strain, speed, fric):
        exx, eyy, exy = strain
        e2 = exx * exx + eyy * eyy + exx * eyy + exy * exy + 0.05
        b2 = 0.25 * fric * fric * (speed[0] * speed[0] + speed[1] * speed[1])
        total_visc = jnp.zeros_like(e2)
        for k in range(total_layers):
            height = 1.0 - (k + 0.5) / total_layers
            total_visc = total_visc + rates[k] * jnp.exp(
                jnp.log(e2 + (height * height) * b2) * (-1.0 / 3.0)
            )
        return thick[...] * (total_visc * (1.0 / total_layers))

    def stresses(strain, visc):
        exx, eyy, exy = strain
        return 2.0 * visc * (2.0 * exx + eyy), 2.0 * visc * (2.0 * eyy + exx), 2.0 * visc * exy

    def new_speed(speed, fric, visc, stress, phase):
        sxx, syy, sxy = stress
        div_0 = diff_rows(sxx, *row_halo(phase, 0)) + diff_cols(sxy, *col_halo(phase, 0))
        div_1 = diff_rows(sxy, *row_halo(phase, 1)) + diff_cols(syy, *col_halo(phase, 1))
        scale = 0.5 * icy / (1.0 + fric + 4.0 * visc)
        return (
            speed[0] + scale * (div_0 - fric * speed[0] + drive[0]),
            speed[1] + scale * (div_1 - fric * speed[1] + drive[1]),
        )

    speed = (vel[0], vel[1])
    coeff = fric_in[...]
    fric = grounded * jnp.exp(coeff)
    strain = strains(
        speed,
        row_halo(0, 0),
        row_halo(0, 1),
        (edge_left[0, :, LANES - 1 : LANES], edge_right[0, :, 0:1]),
        (edge_left[1, :, LANES - 1 : LANES], edge_right[1, :, 0:1]),
    )
    visc = viscosity(strain, speed, fric)
    stress = stresses(strain, visc)
    edges = send_edges(1, (stress[0], stress[2]), (stress[2], stress[1]))

    build(groups - 1, *odd)
    multiply(*even)
    multiply(*odd)

    def collect(q):
        for channel in range(CHANNELS):
            field = None
            for piece in range(PIECES):
                start = pl.multiple_of((channel * PIECES + piece) * marks + q * rows, rows)
                part = total[pl.ds(start, rows), :]
                field = part if field is None else field + part
            fields[q, channel] = field

    sum_copies = []
    for k, chip in enumerate((1 - pair, pair)):
        q = chip * 2 + (1 - core)
        collect(q)
        copy = remote(
            fields.at[q], from_sibling.at[k], sum_send_sems.at[k], sum_recv_sems.at[k], t, sibling
        )
        copy.start()
        sum_copies.append(copy)
    collect(partner)

    sum_copies[0].wait()
    pair_sum[...] = fields[partner] + from_sibling[0]
    cross = remote(pair_sum, from_partner, sum_send_sems.at[2], sum_recv_sems.at[2], t, partner)
    cross.start()
    collect(l)

    for copy in edges:
        copy.wait()
    speed = new_speed(speed, fric, visc, stress, 1)
    edges = send_edges(2, speed, speed)
    sum_copies[1].wait()
    for channel in range(CHANNELS):
        fields[l, channel] = fields[l, channel] + from_sibling[1, channel]
    for copy in edges:
        copy.wait()
    strain = strains(speed, row_halo(2, 0), row_halo(2, 1), col_halo(2, 0), col_halo(2, 1))
    cross.wait()
    weight_sum, seen_0, seen_1 = (fields[l, k] + from_partner[k] for k in range(CHANNELS))

    def new_coeff(coeff, fric, speed):
        along = speed[0] * (weight_sum * speed[0] - seen_0) + speed[1] * (
            weight_sum * speed[1] - seen_1
        )
        return coeff - 0.2 * fric * along

    coeff = new_coeff(coeff, fric, speed)

    fric = grounded * jnp.exp(coeff)
    visc = viscosity(strain, speed, fric)
    stress = stresses(strain, visc)
    for copy in send_edges(3, (stress[0], stress[2]), (stress[2], stress[1])):
        copy.wait()
    speed = new_speed(speed, fric, visc, stress, 3)
    result[0] = speed[0]
    result[1] = speed[1]
    result[2] = new_coeff(coeff, fric, speed)

    own = [
        pltpu.make_async_copy(result.at[0:2], velocity_out.at[:, :, columns], own_sems.at[0]),
        pltpu.make_async_copy(result.at[2], friction_out.at[:, columns], own_sems.at[1]),
    ]
    other = pl.ds(pl.multiple_of(partner * quarter, LANES), quarter)
    sent, crossed, passed = [], [], []
    for k, src in enumerate((result.at[0], result.at[1], result.at[2])):
        dst = friction_out.at[:, columns] if k == 2 else velocity_out.at[k, :, columns]
        copy = remote(src, dst, out_send_sems.at[0, k], out_recv_sems.at[0, k], t, partner)
        copy.start()
        crossed.append(copy)
        copy = remote(src, dst, out_send_sems.at[1, k], out_recv_sems.at[1, k], t, sibling)
        copy.start()
        sent.append(copy)
    for copy in own:
        copy.start()
    for k, copy in enumerate(crossed):
        copy.wait_recv()
        dst = friction_out.at[:, other] if k == 2 else velocity_out.at[k, :, other]
        copy = remote(dst, dst, out_send_sems.at[2, k], out_recv_sems.at[2, k], t, sibling)
        copy.start()
        passed.append(copy)
    for copy in crossed:
        copy.wait_send()
    for copy in own + sent + passed:
        copy.wait()

    pltpu.make_async_copy(
        packed.at[pl.ds(1, n_tile - 1)], packed.at[pl.ds(1, n_tile - 1)], obs_send_sem
    ).wait()


def body(
    velocity,
    friction,
    thickness,
    rate,
    driving,
    ice_mask,
    obs_velocity,
    obs_weight,
    obs_cells,
    obs_counts,
):
    n_tile, n_layer = lax.axis_size("tile"), lax.axis_size("layer")
    rows, width = friction.shape
    quarter = width // n_layer
    slots = obs_weight.shape[-1]
    depth = rate.shape[0]
    sides = (4, n_tile // 8, 2) if n_tile % 8 == 0 else (1, n_tile // 2, 2)
    marks = rows * n_layer
    groups = sides[1]
    chunk = (n_tile // groups) * slots
    in_hbm = pl.BlockSpec(memory_space=pltpu.HBM)
    f32 = jnp.float32
    friction_out, velocity_out = pl.pallas_call(
        functools.partial(kernel, sides, n_layer),
        out_shape=(
            jax.ShapeDtypeStruct(friction.shape, f32),
            jax.ShapeDtypeStruct(velocity.shape, f32),
        ),
        in_specs=[in_hbm] * 10,
        out_specs=(in_hbm, in_hbm),
        scratch_shapes=[
            pltpu.VMEM((n_tile, 4, slots), f32),
            pltpu.VMEM((n_tile, 4, slots), f32),
            [pltpu.VMEM((CHANNELS * PIECES * marks, chunk), jnp.bfloat16)] * 2,
            [pltpu.VMEM((chunk, quarter), jnp.bfloat16)] * 2,
            pltpu.VMEM((CHANNELS * PIECES * marks, quarter), f32),
            pltpu.VMEM((n_layer, CHANNELS, rows, quarter), f32),
            pltpu.VMEM((2, CHANNELS, rows, quarter), f32),
            pltpu.VMEM((CHANNELS, rows, quarter), f32),
            pltpu.VMEM((CHANNELS, rows, quarter), f32),
            pltpu.VMEM((depth * n_layer, rows, quarter), f32),
            pltpu.VMEM((2, rows, quarter), f32),
            pltpu.VMEM((2, rows, LANES), f32),
            pltpu.VMEM((2, rows, LANES), f32),
            pltpu.VMEM((rows, quarter), f32),
            pltpu.VMEM((rows, quarter), f32),
            pltpu.VMEM((2, rows, quarter), f32),
            pltpu.VMEM((rows, quarter), jnp.int32),
            pltpu.VMEM((4, 2, 2, quarter), f32),
            pltpu.VMEM((4, 2, 2, quarter), f32),
            pltpu.VMEM((3, 2, 2, rows, LANES), f32),
            pltpu.VMEM((3, 2, 2, rows, LANES), f32),
            pltpu.VMEM((3, rows, quarter), f32),
            pltpu.VMEM((n_tile, 2 * slots), f32),
            pltpu.VMEM((n_tile, slots), f32),
            pltpu.VMEM((n_tile, slots), jnp.int32),
            pltpu.VMEM((1, n_tile), jnp.int32),
            pltpu.SemaphoreType.DMA((12,)),
            pltpu.SemaphoreType.DMA,
            pltpu.SemaphoreType.DMA((groups,)),
            pltpu.SemaphoreType.DMA((3,)),
            pltpu.SemaphoreType.DMA((3,)),
            pltpu.SemaphoreType.DMA((4, 2)),
            pltpu.SemaphoreType.DMA((4, 2)),
            pltpu.SemaphoreType.DMA((3, 2)),
            pltpu.SemaphoreType.DMA((3, 2)),
            pltpu.SemaphoreType.DMA((3,)),
            pltpu.SemaphoreType.DMA((3,)),
            pltpu.SemaphoreType.DMA((3, 3)),
            pltpu.SemaphoreType.DMA((3, 3)),
            pltpu.SemaphoreType.DMA((2,)),
        ],
        compiler_params=pltpu.CompilerParams(
            collective_id=0, has_side_effects=True, vmem_limit_bytes=VMEM_BYTES
        ),
    )(
        velocity,
        friction,
        thickness,
        rate,
        driving,
        ice_mask,
        obs_velocity.reshape(n_tile, 2 * slots),
        obs_weight.reshape(n_tile, slots),
        obs_cells.reshape(n_tile, slots),
        obs_counts.reshape(1, n_tile),
    )
    return friction_out, velocity_out


def solution(mesh):
    placed = (
        P(None, "tile", None),
        P("tile", None),
        P("tile", None),
        P("layer", "tile", None),
        P(None, "tile", None),
        P("tile", None),
        P("tile", "layer", None, None),
        P("tile", "layer", None, None),
        P("tile", "layer", None, None),
        P("tile", "layer", None),
    )
    return jax.shard_map(
        body,
        mesh=mesh,
        in_specs=placed,
        out_specs=(P("tile", None), P(None, "tile", None)),
        check_vma=False,
    )
```

```python
import functools

import jax
import jax.numpy as jnp
from jax import lax
from jax.experimental import pallas as pl
from jax.experimental.pallas import tpu as pltpu
from jax.sharding import PartitionSpec as P

ITERS = 2
MESH = pl.DeviceIdType.MESH
LANES = 128
PIECES = 3
VMEM_BYTES = 58 * 1024 * 1024
IT1_AT = 1

CHANNELS = 3


def split_pieces(value):
    pieces = []
    for _ in range(PIECES):
        piece = value.astype(jnp.bfloat16).astype(jnp.float32)
        pieces.append(piece)
        value = value - piece
    return pieces


def kernel(
    sides,
    n_layer,
    velocity,
    friction,
    thickness,
    rate,
    driving,
    ice_mask,
    obs_velocity,
    obs_weight,
    obs_cells,
    obs_counts,
    friction_out,
    velocity_out,
    packed,
    received,
    left_sides,
    right_sides,
    total,
    fields,
    from_sibling,
    chip_sum,
    other_sum,
    along_send,
    along_recv,
    rates,
    vel,
    edge,
    fric_in,
    thick,
    drive,
    mask,
    part_send,
    part_recv,
    row_send,
    row_recv,
    col_send,
    col_recv,
    result,
    seen_in,
    weight_in,
    cells_in,
    counts_in,
    load_sems,
    obs_send_sem,
    obs_recv_sems,
    rate_sems,
    part_send_sems,
    part_recv_sems,
    row_send_sems,
    row_recv_sems,
    col_send_sems,
    col_recv_sems,
    sum_send_sems,
    sum_recv_sems,
    out_send_sems,
    out_recv_sems,
    own_sems,
):
    n_x, groups, n_y = sides
    per_group = n_x * n_y
    n_tile = groups * per_group
    t = lax.axis_index("tile")
    l = lax.axis_index("layer")
    rows, width = friction.shape
    half = width // 2
    quarter = width // n_layer
    depth = rate.shape[0]
    total_layers = depth * n_layer
    slots = obs_weight.shape[-1]
    marks = rows * n_layer
    core = lax.rem(l, 2)
    chip = l // 2
    sibling = chip * 2 + (1 - core)
    partner = (1 - chip) * 2 + core
    across = (1 - chip) * 2 + (1 - core)
    above = lax.rem(t + n_tile - 1, n_tile)
    below = lax.rem(t + 1, n_tile)
    first = pl.multiple_of(core * half, LANES)
    columns = pl.ds(first, half)
    sibling_columns = pl.ds(pl.multiple_of((1 - core) * half, LANES), half)

    def remote(src, dst, send_sem, recv_sem, tile, layer):
        return pltpu.make_async_remote_copy(
            src_ref=src,
            dst_ref=dst,
            send_sem=send_sem,
            recv_sem=recv_sem,
            device_id=(tile, layer),
            device_id_type=MESH,
        )

    beside = pl.multiple_of(half - LANES * core, LANES)
    loads = [
        pltpu.make_async_copy(obs_velocity, seen_in, load_sems.at[0]),
        pltpu.make_async_copy(obs_weight, weight_in, load_sems.at[1]),
        pltpu.make_async_copy(obs_cells, cells_in, load_sems.at[2]),
        pltpu.make_async_copy(obs_counts, counts_in, load_sems.at[3]),
        pltpu.make_async_copy(velocity.at[:, :, columns], vel, load_sems.at[4]),
        pltpu.make_async_copy(velocity.at[:, :, pl.ds(beside, LANES)], edge, load_sems.at[5]),
        pltpu.make_async_copy(friction.at[:, columns], fric_in, load_sems.at[6]),
        pltpu.make_async_copy(thickness.at[:, columns], thick, load_sems.at[7]),
        pltpu.make_async_copy(driving.at[:, :, columns], drive, load_sems.at[8]),
        pltpu.make_async_copy(ice_mask.at[:, columns], mask, load_sems.at[9]),
        pltpu.make_async_copy(
            rate.at[:, :, columns], rates.at[pl.ds(core * depth, depth)], load_sems.at[10]
        ),
    ]
    for load in loads:
        load.start()

    barrier = pltpu.get_barrier_semaphore()
    x, z, y = t // (groups * n_y), lax.rem(t // n_y, groups), lax.rem(t, n_y)

    def peer(turn):
        ring = turn // per_group
        step = lax.rem(ring, 2)
        hop = step * ((ring + 1) // 2) + (1 - step) * (groups - ring // 2)
        to_x = lax.rem(x + lax.rem(turn // n_y, n_x), n_x)
        to_z = lax.rem(z + hop, groups)
        to_y = lax.rem(y + turn, n_y)
        return (to_x * groups + to_z) * n_y + to_y

    def greet_one(tile, layer):
        pl.semaphore_signal(barrier, inc=1, device_id=(tile, layer), device_id_type=MESH)

    def greet(turn, carry):
        greet_one(peer(n_tile - turn), l)
        return carry

    lax.fori_loop(1, n_tile, greet, 0)
    greet_one(above, partner)
    greet_one(below, partner)
    for layer in (partner, across, sibling):
        greet_one(t, layer)

    for load in loads[:4]:
        load.wait()
    row_id = lax.broadcasted_iota(jnp.int32, (n_tile, n_tile), 0)
    col_id = lax.broadcasted_iota(jnp.int32, (n_tile, n_tile), 1)
    counts = jnp.sum(
        jnp.where(row_id == col_id, counts_in[...].astype(jnp.float32), 0.0), axis=1, keepdims=True
    )
    place = lax.broadcasted_iota(jnp.int32, (n_tile, slots), 1).astype(jnp.float32)
    weight = jnp.where(place < counts, weight_in[...], 0.0)
    packed[:, 0, :] = weight
    packed[:, 1, :] = weight * seen_in[:, :slots]
    packed[:, 2, :] = weight * seen_in[:, slots:]
    packed[:, 3, :] = cells_in[...].astype(jnp.float32)

    for load in loads[4:6]:
        load.wait()
    row_send[0, 0] = vel[:, 0, :]
    row_send[0, 1] = vel[:, rows - 1, :]

    pl.semaphore_wait(barrier, n_tile - 1 + 2 + n_layer - 1)

    def row_copies(phase):
        copies = []
        for side, tile in ((0, above), (1, below)):
            for source, layer in enumerate((l, partner) if phase % 2 else (l,)):
                copies.append(
                    remote(
                        row_send.at[phase, side],
                        row_recv.at[phase, 1 - side, source],
                        row_send_sems.at[phase, side, source],
                        row_recv_sems.at[phase, 1 - side, source],
                        tile,
                        layer,
                    )
                )
        return copies

    def col_copies(phase):
        return [
            remote(
                col_send.at[phase - 1],
                col_recv.at[phase - 1, source],
                col_send_sems.at[phase - 1, source],
                col_recv_sems.at[phase - 1, source],
                t,
                layer,
            )
            for source, layer in enumerate((sibling, across) if phase % 2 else (sibling,))
        ]

    def part_copy(turn):
        return remote(
            part_send.at[turn],
            part_recv.at[turn],
            part_send_sems.at[turn],
            part_recv_sems.at[turn],
            t,
            partner,
        )

    def start(copies):
        for copy in copies:
            copy.start()

    def wait(copies):
        for copy in copies:
            copy.wait()

    start(row_copies(0))
    own_block = pltpu.make_async_copy(packed.at[t], received.at[0], obs_recv_sems.at[0])
    own_block.start()

    def send_obs(turn, carry):
        to = peer(turn)
        remote(
            packed.at[to],
            received.at[turn],
            obs_send_sem,
            obs_recv_sems.at[turn // per_group],
            to,
            l,
        ).start()
        return carry

    lax.fori_loop(1, n_tile, send_obs, 0)
    rate_copy = remote(
        rate.at[:, :, sibling_columns],
        rates.at[pl.ds(core * depth, depth)],
        rate_sems.at[0],
        rate_sems.at[1],
        t,
        sibling,
    )
    rate_copy.start()

    row_of = lax.broadcasted_iota(jnp.int32, (rows, half), 0)
    col_of = lax.broadcasted_iota(jnp.int32, (rows, half), 1)
    top, bottom = t == 0, t == n_tile - 1
    at_left = core == 0

    def diff_rows(field, low, high):
        low = jnp.where(top, 0.0, low)
        high = jnp.where(bottom, 0.0, high)
        previous = jnp.where(row_of == 0, low, pltpu.roll(field, 1, 0))
        following = jnp.where(row_of == rows - 1, high, pltpu.roll(field, rows - 1, 0))
        return 0.5 * (following - previous)

    def diff_cols(field, tile):
        low = jnp.where(at_left, 0.0, tile[:, LANES - 1 : LANES])
        high = jnp.where(at_left, tile[:, 0:1], 0.0)
        previous = jnp.where(col_of == 0, low, pltpu.roll(field, 1, 1))
        following = jnp.where(col_of == half - 1, high, pltpu.roll(field, half - 1, 1))
        return 0.5 * (following - previous)

    def row_halo(phase, k):
        low, high = row_recv[phase, 0, 0, k : k + 1, :], row_recv[phase, 1, 0, k : k + 1, :]
        if phase % 2:
            low = low + row_recv[phase, 0, 1, k : k + 1, :]
            high = high + row_recv[phase, 1, 1, k : k + 1, :]
        return low, high

    def col_halo(phase, k):
        tile = col_recv[phase - 1, 0, k]
        return tile + col_recv[phase - 1, 1, k] if phase % 2 else tile

    def stage(phase, by_row, by_col):
        for k in range(2):
            row_send[phase, 0, k : k + 1, :] = by_row[k][0:1, :]
            row_send[phase, 1, k : k + 1, :] = by_row[k][rows - 1 : rows, :]
            col_send[phase - 1, k] = jnp.where(
                at_left, by_col[k][:, half - LANES :], by_col[k][:, :LANES]
            )

    def strains(speed, phase, tiles):
        exx = diff_rows(speed[0], *row_halo(phase, 0))
        eyy = diff_cols(speed[1], tiles[1])
        exy = 0.5 * (diff_cols(speed[0], tiles[0]) + diff_rows(speed[1], *row_halo(phase, 1)))
        return exx, eyy, exy

    def stresses(strain, visc):
        exx, eyy, exy = strain
        return 2.0 * visc * (2.0 * exx + eyy), 2.0 * visc * (2.0 * eyy + exx), 2.0 * visc * exy

    chip_layers = 2 * depth
    first_layer = (chip * chip_layers).astype(jnp.float32)

    def send_part(turn, strain, speed, fric):
        exx, eyy, exy = strain
        e2 = exx * exx + eyy * eyy + exx * eyy + exy * exy + 0.05
        b2 = 0.25 * fric * fric * (speed[0] * speed[0] + speed[1] * speed[1])
        layer_sum = jnp.zeros_like(e2)
        for k in range(chip_layers):
            height = 1.0 - (first_layer + (k + 0.5)) * (1.0 / total_layers)
            layer_sum = layer_sum + rates[k] * jnp.exp(
                jnp.log(e2 + (height * height) * b2) * (-1.0 / 3.0)
            )
        part = thick[...] * (layer_sum * (1.0 / total_layers))
        part_send[turn] = part
        sxx, syy, sxy = stresses(strain, part)
        phase = 2 * turn + 1
        stage(phase, (sxx, sxy), (sxy, syy))
        start(row_copies(phase))
        part_copy(turn).start()
        start(col_copies(phase))

    def new_speed(turn, strain, speed, fric):
        phase = 2 * turn + 1
        wait(row_copies(phase) + [part_copy(turn)] + col_copies(phase))
        visc = part_send[turn] + part_recv[turn]
        sxx, syy, sxy = stresses(strain, visc)
        div_0 = diff_rows(sxx, *row_halo(phase, 0)) + diff_cols(sxy, col_halo(phase, 0))
        div_1 = diff_rows(sxy, *row_halo(phase, 1)) + diff_cols(syy, col_halo(phase, 1))
        icy = jnp.where(mask[...] >= 1, 1.0, 0.0)
        scale = 0.5 * icy / (1.0 + fric + 4.0 * visc)
        return (
            speed[0] + scale * (div_0 - fric * speed[0] + drive[0]),
            speed[1] + scale * (div_1 - fric * speed[1] + drive[1]),
        )

    def drag(coeff):
        return jnp.where(mask[...] == 2, 1.0, 0.0) * jnp.exp(coeff)

    def first_state():
        speed = (vel[0], vel[1])
        return strains(speed, 0, (edge[0], edge[1])), speed, drag(fric_in[...])

    def first_part():
        wait(loads[6:])
        rate_copy.wait()
        wait(row_copies(0))
        send_part(0, *first_state())

    total[...] = jnp.zeros_like(total)
    mark_id = lax.broadcasted_iota(jnp.int32, (marks, slots), 0).astype(jnp.float32)
    lane_id = lax.broadcasted_iota(jnp.int32, (slots, quarter), 1).astype(jnp.float32)

    def arrive(group):
        blocks = received.at[pl.ds(group * per_group, per_group)]
        pltpu.make_async_copy(blocks, blocks, obs_recv_sems.at[group]).wait()

    def build(group, left_side, right_side):
        block = received[pl.ds(group * per_group, per_group)]
        cell = block[:, 3, :]
        mark = jnp.floor((cell + 0.5) * (1.0 / quarter))
        column = cell - mark * quarter
        row = jnp.floor((mark + 0.5) * (1.0 / n_layer))
        mark = (mark - row * n_layer) * rows + row
        column = column.T
        pieces = []
        for channel in range(CHANNELS):
            pieces += split_pieces(block[:, channel, :])
        for b in range(per_group):
            hit = mark[b : b + 1, :] == mark_id
            for p, piece in enumerate(pieces):
                left_side[p * marks : (p + 1) * marks, b * slots : (b + 1) * slots] = jnp.where(
                    hit, piece[b : b + 1, :], 0.0
                ).astype(jnp.bfloat16)
            right_side[b * slots : (b + 1) * slots, :] = jnp.where(
                column[:, b : b + 1] == lane_id, 1.0, 0.0
            ).astype(jnp.bfloat16)

    def multiply(left_side, right_side):
        total[...] += jnp.dot(left_side[...], right_side[...], preferred_element_type=jnp.float32)

    even, odd = (left_sides[0], right_sides[0]), (left_sides[1], right_sides[1])
    turns = groups // 2

    def two_groups(turn, carry):
        arrive(2 * turn + 1)
        pl.when(turn < turns - 1)(lambda: arrive(2 * turn + 2))
        pl.when(turn == min(IT1_AT, turns - 1))(first_part)
        build(2 * turn + 1, *odd)
        multiply(*even)
        build(lax.rem(2 * turn + 2, groups), *even)
        multiply(*odd)
        return carry

    arrive(0)
    build(0, *even)
    lax.fori_loop(0, turns, two_groups, 0)

    def collect(side):
        for channel in range(CHANNELS):
            for q in range(2):
                field = None
                for piece in range(PIECES):
                    at = (channel * PIECES + piece) * marks + (side * 2 + q) * rows
                    part = total[pl.ds(pl.multiple_of(at, rows), rows), :]
                    field = part if field is None else field + part
                fields[side, channel, :, q * quarter : (q + 1) * quarter] = field

    collect(1 - core)
    sum_copy = remote(
        fields.at[1 - core], from_sibling, sum_send_sems.at[0], sum_recv_sems.at[0], t, sibling
    )
    sum_copy.start()
    collect(core)

    strain, speed, fric = first_state()
    speed = new_speed(0, strain, speed, fric)
    stage(2, speed, speed)
    swaps = row_copies(2) + col_copies(2)
    start(swaps)

    def misfit(sums, speed):
        return speed[0] * (sums[0] * speed[0] - sums[1]) + speed[1] * (
            sums[0] * speed[1] - sums[2]
        )

    sum_copy.wait()
    sums = [fields[core, k] + from_sibling[k] for k in range(CHANNELS)]
    for k in range(CHANNELS):
        chip_sum[k] = sums[k]
    along_send[...] = misfit(sums, speed)
    along_copy = remote(
        along_send, along_recv, sum_send_sems.at[1], sum_recv_sems.at[1], t, partner
    )
    along_copy.start()
    chip_copy = remote(chip_sum, other_sum, sum_send_sems.at[2], sum_recv_sems.at[2], t, partner)
    chip_copy.start()
    wait(swaps)
    strain = strains(speed, 2, (col_halo(2, 0), col_halo(2, 1)))
    along_copy.wait()
    coeff = fric_in[...] - 0.2 * fric * (along_send[...] + along_recv[...])

    fric = drag(coeff)
    send_part(1, strain, speed, fric)
    speed = new_speed(1, strain, speed, fric)
    result[0] = speed[0]
    result[1] = speed[1]
    chip_copy.wait()
    sums = [chip_sum[k] + other_sum[k] for k in range(CHANNELS)]
    result[2] = coeff - 0.2 * fric * misfit(sums, speed)

    finals = []
    for k, dst in ((0, velocity_out.at[:, :, columns]), (1, friction_out.at[:, columns])):
        src = result.at[0:2] if k == 0 else result.at[2]
        finals.append(
            remote(src, dst, out_send_sems.at[k], out_recv_sems.at[k], t, sibling)
        )
        finals.append(pltpu.make_async_copy(src, dst, own_sems.at[k]))
    start(finals)
    wait(finals)

    blocks = packed.at[pl.ds(1, n_tile - 1)]
    pltpu.make_async_copy(blocks, blocks, obs_send_sem).wait()


def body(
    velocity,
    friction,
    thickness,
    rate,
    driving,
    ice_mask,
    obs_velocity,
    obs_weight,
    obs_cells,
    obs_counts,
):
    n_tile, n_layer = lax.axis_size("tile"), lax.axis_size("layer")
    rows, width = friction.shape
    half, quarter = width // 2, width // n_layer
    slots = obs_weight.shape[-1]
    depth = rate.shape[0]
    sides = (4, n_tile // 8, 2) if n_tile % 8 == 0 else (1, n_tile // 2, 2)
    marks = rows * n_layer
    groups = sides[1]
    chunk = (n_tile // groups) * slots
    in_hbm = pl.BlockSpec(memory_space=pltpu.HBM)
    f32 = jnp.float32
    friction_out, velocity_out = pl.pallas_call(
        functools.partial(kernel, sides, n_layer),
        out_shape=(
            jax.ShapeDtypeStruct(friction.shape, f32),
            jax.ShapeDtypeStruct(velocity.shape, f32),
        ),
        in_specs=[in_hbm] * 10,
        out_specs=(in_hbm, in_hbm),
        scratch_shapes=[
            pltpu.VMEM((n_tile, 4, slots), f32),
            pltpu.VMEM((n_tile, 4, slots), f32),
            [pltpu.VMEM((CHANNELS * PIECES * marks, chunk), jnp.bfloat16)] * 2,
            [pltpu.VMEM((chunk, quarter), jnp.bfloat16)] * 2,
            pltpu.VMEM((CHANNELS * PIECES * marks, quarter), f32),
            pltpu.VMEM((2, CHANNELS, rows, half), f32),
            pltpu.VMEM((CHANNELS, rows, half), f32),
            pltpu.VMEM((CHANNELS, rows, half), f32),
            pltpu.VMEM((CHANNELS, rows, half), f32),
            pltpu.VMEM((rows, half), f32),
            pltpu.VMEM((rows, half), f32),
            pltpu.VMEM((2 * depth, rows, half), f32),
            pltpu.VMEM((2, rows, half), f32),
            pltpu.VMEM((2, rows, LANES), f32),
            pltpu.VMEM((rows, half), f32),
            pltpu.VMEM((rows, half), f32),
            pltpu.VMEM((2, rows, half), f32),
            pltpu.VMEM((rows, half), jnp.int32),
            pltpu.VMEM((2, rows, half), f32),
            pltpu.VMEM((2, rows, half), f32),
            pltpu.VMEM((4, 2, 2, half), f32),
            pltpu.VMEM((4, 2, 2, 2, half), f32),
            pltpu.VMEM((3, 2, rows, LANES), f32),
            pltpu.VMEM((3, 2, 2, rows, LANES), f32),
            pltpu.VMEM((3, rows, half), f32),
            pltpu.VMEM((n_tile, 2 * slots), f32),
            pltpu.VMEM((n_tile, slots), f32),
            pltpu.VMEM((n_tile, slots), jnp.int32),
            pltpu.VMEM((1, n_tile), jnp.int32),
            pltpu.SemaphoreType.DMA((11,)),
            pltpu.SemaphoreType.DMA,
            pltpu.SemaphoreType.DMA((groups,)),
            pltpu.SemaphoreType.DMA((2,)),
            pltpu.SemaphoreType.DMA((2,)),
            pltpu.SemaphoreType.DMA((2,)),
            pltpu.SemaphoreType.DMA((4, 2, 2)),
            pltpu.SemaphoreType.DMA((4, 2, 2)),
            pltpu.SemaphoreType.DMA((3, 2)),
            pltpu.SemaphoreType.DMA((3, 2)),
            pltpu.SemaphoreType.DMA((3,)),
            pltpu.SemaphoreType.DMA((3,)),
            pltpu.SemaphoreType.DMA((2,)),
            pltpu.SemaphoreType.DMA((2,)),
            pltpu.SemaphoreType.DMA((2,)),
        ],
        compiler_params=pltpu.CompilerParams(
            collective_id=0, has_side_effects=True, vmem_limit_bytes=VMEM_BYTES
        ),
    )(
        velocity,
        friction,
        thickness,
        rate,
        driving,
        ice_mask,
        obs_velocity.reshape(n_tile, 2 * slots),
        obs_weight.reshape(n_tile, slots),
        obs_cells.reshape(n_tile, slots),
        obs_counts.reshape(1, n_tile),
    )
    return friction_out, velocity_out


def solution(mesh):
    placed = (
        P(None, "tile", None),
        P("tile", None),
        P("tile", None),
        P("layer", "tile", None),
        P(None, "tile", None),
        P("tile", None),
        P("tile", "layer", None, None),
        P("tile", "layer", None, None),
        P("tile", "layer", None, None),
        P("tile", "layer", None),
    )
    return jax.shard_map(
        body,
        mesh=mesh,
        in_specs=placed,
        out_specs=(P("tile", None), P(None, "tile", None)),
        check_vma=False,
    )
```

```python
import functools

import jax
import jax.numpy as jnp
from jax import lax
from jax.experimental import pallas as pl
from jax.experimental.pallas import tpu as pltpu
from jax.sharding import PartitionSpec as P

ITERS = 2
MESH = pl.DeviceIdType.MESH
LANES = 128
PIECES = 3
VMEM_BYTES = 58 * 1024 * 1024
IT1_AT = 1

CHANNELS = 3


def split_pieces(value):
    pieces = []
    for _ in range(PIECES):
        piece = value.astype(jnp.bfloat16).astype(jnp.float32)
        pieces.append(piece)
        value = value - piece
    return pieces


def kernel(
    sides,
    n_layer,
    velocity,
    friction,
    thickness,
    rate,
    driving,
    ice_mask,
    obs_velocity,
    obs_weight,
    obs_cells,
    obs_counts,
    friction_out,
    velocity_out,
    packed,
    received,
    left_sides,
    right_sides,
    totals,
    fields,
    from_sibling,
    chip_sum,
    other_sum,
    along_send,
    along_recv,
    rates,
    vel,
    edge,
    fric_in,
    thick,
    drive,
    mask,
    part_send,
    part_recv,
    row_send,
    row_recv,
    col_send,
    col_recv,
    seen_in,
    weight_in,
    cells_in,
    counts_in,
    load_sems,
    obs_send_sem,
    obs_recv_sems,
    rate_sems,
    part_send_sems,
    part_recv_sems,
    row_send_sems,
    row_recv_sems,
    col_send_sems,
    col_recv_sems,
    sum_send_sems,
    sum_recv_sems,
    out_send_sems,
    out_recv_sems,
):
    n_x, groups, n_y = sides
    per_group = n_x * n_y
    n_tile = groups * per_group
    t = lax.axis_index("tile")
    l = lax.axis_index("layer")
    rows, width = friction.shape
    half = width // 2
    quarter = width // n_layer
    depth = rate.shape[0]
    total_layers = depth * n_layer
    slots = obs_weight.shape[-1]
    marks = rows * n_layer
    side_marks = CHANNELS * PIECES * marks // 2
    core = lax.rem(l, 2)
    chip = l // 2
    sibling = chip * 2 + (1 - core)
    partner = (1 - chip) * 2 + core
    across = (1 - chip) * 2 + (1 - core)
    above = lax.rem(t + n_tile - 1, n_tile)
    below = lax.rem(t + 1, n_tile)
    first = pl.multiple_of(core * half, LANES)
    columns = pl.ds(first, half)
    sibling_columns = pl.ds(pl.multiple_of((1 - core) * half, LANES), half)

    def remote(src, dst, send_sem, recv_sem, tile, layer):
        return pltpu.make_async_remote_copy(
            src_ref=src,
            dst_ref=dst,
            send_sem=send_sem,
            recv_sem=recv_sem,
            device_id=(tile, layer),
            device_id_type=MESH,
        )

    beside = pl.multiple_of(half - LANES * core, LANES)
    loads = [
        pltpu.make_async_copy(obs_velocity, seen_in, load_sems.at[0]),
        pltpu.make_async_copy(obs_weight, weight_in, load_sems.at[1]),
        pltpu.make_async_copy(obs_cells, cells_in, load_sems.at[2]),
        pltpu.make_async_copy(obs_counts, counts_in, load_sems.at[3]),
        pltpu.make_async_copy(velocity.at[:, :, columns], vel, load_sems.at[4]),
        pltpu.make_async_copy(velocity.at[:, :, pl.ds(beside, LANES)], edge, load_sems.at[5]),
        pltpu.make_async_copy(friction.at[:, columns], fric_in, load_sems.at[6]),
        pltpu.make_async_copy(thickness.at[:, columns], thick, load_sems.at[7]),
        pltpu.make_async_copy(driving.at[:, :, columns], drive, load_sems.at[8]),
        pltpu.make_async_copy(ice_mask.at[:, columns], mask, load_sems.at[9]),
        pltpu.make_async_copy(
            rate.at[:, :, columns], rates.at[pl.ds(core * depth, depth)], load_sems.at[10]
        ),
    ]
    for load in loads:
        load.start()

    barrier = pltpu.get_barrier_semaphore()
    x, z, y = t // (groups * n_y), lax.rem(t // n_y, groups), lax.rem(t, n_y)

    along_x = [lax.rem(x + k, n_x) * (groups * n_y) for k in range(n_x)]
    along_y = [lax.rem(y + k, n_y) for k in range(n_y)]

    def ring_of(ring):
        odd_ring = lax.rem(ring, 2)
        hop = odd_ring * ((ring + 1) // 2) + (1 - odd_ring) * (groups - ring // 2)
        to_z = lax.rem(z + hop, groups) * n_y
        return [to_x + to_z + to_y for to_x in along_x for to_y in along_y]

    def greet_one(tile, layer):
        pl.semaphore_signal(barrier, inc=1, device_id=(tile, layer), device_id_type=MESH)

    def greet(turn, carry):
        for tile in ring_of(groups - turn):
            greet_one(tile, l)
        return carry

    lax.fori_loop(1, groups, greet, 0)
    for tile in ring_of(0)[1:]:
        greet_one(tile, l)
    greet_one(above, partner)
    greet_one(below, partner)
    for layer in (partner, across, sibling):
        greet_one(t, layer)

    for load in loads[:4]:
        load.wait()
    row_id = lax.broadcasted_iota(jnp.int32, (n_tile, n_tile), 0)
    col_id = lax.broadcasted_iota(jnp.int32, (n_tile, n_tile), 1)
    counts = jnp.sum(
        jnp.where(row_id == col_id, counts_in[...].astype(jnp.float32), 0.0), axis=1, keepdims=True
    )
    place = lax.broadcasted_iota(jnp.int32, (n_tile, slots), 1).astype(jnp.float32)
    weight = jnp.where(place < counts, weight_in[...], 0.0)
    packed[:, 0, :] = weight
    packed[:, 1, :] = weight * seen_in[:, :slots]
    packed[:, 2, :] = weight * seen_in[:, slots:]
    packed[:, 3, :] = cells_in[...].astype(jnp.float32)

    for load in loads[4:6]:
        load.wait()
    row_send[0, 0] = vel[:, 0, :]
    row_send[0, 1] = vel[:, rows - 1, :]

    pl.semaphore_wait(barrier, n_tile - 1 + 2 + n_layer - 1)

    def row_copies(phase):
        copies = []
        for side, tile in ((0, above), (1, below)):
            for source, layer in enumerate((l, partner) if phase % 2 else (l,)):
                copies.append(
                    remote(
                        row_send.at[phase, side],
                        row_recv.at[phase, 1 - side, source],
                        row_send_sems.at[phase, side, source],
                        row_recv_sems.at[phase, 1 - side, source],
                        tile,
                        layer,
                    )
                )
        return copies

    def col_copies(phase):
        return [
            remote(
                col_send.at[phase - 1],
                col_recv.at[phase - 1, source],
                col_send_sems.at[phase - 1, source],
                col_recv_sems.at[phase - 1, source],
                t,
                layer,
            )
            for source, layer in enumerate((sibling, across) if phase % 2 else (sibling,))
        ]

    def part_copy(turn):
        return remote(
            part_send.at[turn],
            part_recv.at[turn],
            part_send_sems.at[turn],
            part_recv_sems.at[turn],
            t,
            partner,
        )

    def start(copies):
        for copy in copies:
            copy.start()

    def wait(copies):
        for copy in copies:
            copy.wait()

    start(row_copies(0))
    own_block = pltpu.make_async_copy(packed.at[t], received.at[0], obs_recv_sems.at[0])
    own_block.start()

    def send_obs(tile, ring, k):
        remote(
            packed.at[tile],
            received.at[ring * per_group + k],
            obs_send_sem,
            obs_recv_sems.at[ring],
            tile,
            l,
        ).start()

    def send_ring(ring, carry):
        for k, tile in enumerate(ring_of(ring)):
            send_obs(tile, ring, k)
        return carry

    for k, tile in enumerate(ring_of(0)):
        if k > 0:
            send_obs(tile, 0, k)
    lax.fori_loop(1, groups, send_ring, 0)
    rate_copy = remote(
        rate.at[:, :, sibling_columns],
        rates.at[pl.ds(core * depth, depth)],
        rate_sems.at[0],
        rate_sems.at[1],
        t,
        sibling,
    )
    rate_copy.start()

    row_of = lax.broadcasted_iota(jnp.int32, (rows, half), 0)
    col_of = lax.broadcasted_iota(jnp.int32, (rows, half), 1)
    top, bottom = t == 0, t == n_tile - 1
    at_left = core == 0

    def diff_rows(field, low, high):
        low = jnp.where(top, 0.0, low)
        high = jnp.where(bottom, 0.0, high)
        previous = jnp.where(row_of == 0, low, pltpu.roll(field, 1, 0))
        following = jnp.where(row_of == rows - 1, high, pltpu.roll(field, rows - 1, 0))
        return 0.5 * (following - previous)

    def diff_cols(field, tile):
        low = jnp.where(at_left, 0.0, tile[:, LANES - 1 : LANES])
        high = jnp.where(at_left, tile[:, 0:1], 0.0)
        previous = jnp.where(col_of == 0, low, pltpu.roll(field, 1, 1))
        following = jnp.where(col_of == half - 1, high, pltpu.roll(field, half - 1, 1))
        return 0.5 * (following - previous)

    def row_halo(phase, k):
        low, high = row_recv[phase, 0, 0, k : k + 1, :], row_recv[phase, 1, 0, k : k + 1, :]
        if phase % 2:
            low = low + row_recv[phase, 0, 1, k : k + 1, :]
            high = high + row_recv[phase, 1, 1, k : k + 1, :]
        return low, high

    def col_halo(phase, k):
        tile = col_recv[phase - 1, 0, k]
        return tile + col_recv[phase - 1, 1, k] if phase % 2 else tile

    def stage(phase, by_row, by_col):
        for k in range(2):
            row_send[phase, 0, k : k + 1, :] = by_row[k][0:1, :]
            row_send[phase, 1, k : k + 1, :] = by_row[k][rows - 1 : rows, :]
            col_send[phase - 1, k] = jnp.where(
                at_left, by_col[k][:, half - LANES :], by_col[k][:, :LANES]
            )

    def strains(speed, phase, tiles):
        exx = diff_rows(speed[0], *row_halo(phase, 0))
        eyy = diff_cols(speed[1], tiles[1])
        exy = 0.5 * (diff_cols(speed[0], tiles[0]) + diff_rows(speed[1], *row_halo(phase, 1)))
        return exx, eyy, exy

    def stresses(strain, visc):
        exx, eyy, exy = strain
        return 2.0 * visc * (2.0 * exx + eyy), 2.0 * visc * (2.0 * eyy + exx), 2.0 * visc * exy

    chip_layers = 2 * depth
    first_layer = (chip * chip_layers).astype(jnp.float32)

    def send_part(turn, strain, speed, fric):
        exx, eyy, exy = strain
        e2 = exx * exx + eyy * eyy + exx * eyy + exy * exy + 0.05
        b2 = 0.25 * fric * fric * (speed[0] * speed[0] + speed[1] * speed[1])
        layer_sum = jnp.zeros_like(e2)
        for k in range(chip_layers):
            height = 1.0 - (first_layer + (k + 0.5)) * (1.0 / total_layers)
            layer_sum = layer_sum + rates[k] * jnp.exp(
                jnp.log(e2 + (height * height) * b2) * (-1.0 / 3.0)
            )
        part = thick[...] * (layer_sum * (1.0 / total_layers))
        part_send[turn] = part
        sxx, syy, sxy = stresses(strain, part)
        phase = 2 * turn + 1
        stage(phase, (sxx, sxy), (sxy, syy))
        start(row_copies(phase))
        part_copy(turn).start()
        start(col_copies(phase))

    def new_speed(turn, strain, speed, fric):
        phase = 2 * turn + 1
        wait(row_copies(phase) + [part_copy(turn)] + col_copies(phase))
        visc = part_send[turn] + part_recv[turn]
        sxx, syy, sxy = stresses(strain, visc)
        div_0 = diff_rows(sxx, *row_halo(phase, 0)) + diff_cols(sxy, col_halo(phase, 0))
        div_1 = diff_rows(sxy, *row_halo(phase, 1)) + diff_cols(syy, col_halo(phase, 1))
        icy = jnp.where(mask[...] >= 1, 1.0, 0.0)
        scale = 0.5 * icy / (1.0 + fric + 4.0 * visc)
        return (
            speed[0] + scale * (div_0 - fric * speed[0] + drive[0]),
            speed[1] + scale * (div_1 - fric * speed[1] + drive[1]),
        )

    def drag(coeff):
        return jnp.where(mask[...] == 2, 1.0, 0.0) * jnp.exp(coeff)

    def first_state():
        speed = (vel[0], vel[1])
        return strains(speed, 0, (edge[0], edge[1])), speed, drag(fric_in[...])

    def first_part():
        wait(loads[6:])
        rate_copy.wait()
        wait(row_copies(0))
        send_part(0, *first_state())

    for total in totals:
        total[...] = jnp.zeros_like(total)
    mark_id = lax.broadcasted_iota(jnp.int32, (marks, slots), 0).astype(jnp.float32)
    lane_id = lax.broadcasted_iota(jnp.int32, (slots, quarter), 1).astype(jnp.float32)

    def arrive(group):
        blocks = received.at[pl.ds(group * per_group, per_group)]
        pltpu.make_async_copy(blocks, blocks, obs_recv_sems.at[group]).wait()

    def build(group, left_side, right_side):
        block = received[pl.ds(group * per_group, per_group)]
        cell = block[:, 3, :]
        mark = jnp.floor((cell + 0.5) * (1.0 / quarter))
        column = cell - mark * quarter
        row = jnp.floor((mark + 0.5) * (1.0 / n_layer))
        mark = (mark - row * n_layer) * rows + row
        column = column.T
        pieces = []
        for channel in range(CHANNELS):
            pieces += split_pieces(block[:, channel, :])
        for b in range(per_group):
            hit = mark[b : b + 1, :] == mark_id
            for p, piece in enumerate(pieces):
                marked = jnp.where(hit, piece[b : b + 1, :], 0.0).astype(jnp.bfloat16)
                for side in range(2):
                    at = side * side_marks + p * (marks // 2)
                    left_side[at : at + marks // 2, b * slots : (b + 1) * slots] = marked[
                        side * (marks // 2) : (side + 1) * (marks // 2)
                    ]
            right_side[b * slots : (b + 1) * slots, :] = jnp.where(
                column[:, b : b + 1] == lane_id, 1.0, 0.0
            ).astype(jnp.bfloat16)

    def multiply(left_side, right_side, total):
        total[...] += jnp.dot(left_side[...], right_side[...], preferred_element_type=jnp.float32)

    def multiply_side(side, left_side, right_side, total):
        part = pl.ds(pl.multiple_of(side * side_marks, side_marks), side_marks)
        total[part, :] += jnp.dot(
            left_side[part, :], right_side[...], preferred_element_type=jnp.float32
        )

    even = (left_sides[0], right_sides[0], totals[0])
    odd = (left_sides[1], right_sides[1], totals[1])
    turns = groups // 2 - 1

    def two_groups(turn, carry):
        arrive(2 * turn + 1)
        arrive(2 * turn + 2)
        pl.when(turn == min(IT1_AT, turns - 1))(first_part)
        build(2 * turn + 1, *odd[:2])
        multiply(*even)
        build(2 * turn + 2, *even[:2])
        multiply(*odd)
        return carry

    def collect(side):
        for channel in range(CHANNELS):
            for q in range(2):
                field = None
                for piece in range(PIECES):
                    at = side * side_marks + ((channel * PIECES + piece) * 2 + q) * rows
                    part = pl.ds(pl.multiple_of(at, rows), rows)
                    value = totals[0][part, :] + totals[1][part, :]
                    field = value if field is None else field + value
                fields[side, channel, :, q * quarter : (q + 1) * quarter] = field

    arrive(0)
    build(0, *even[:2])
    lax.fori_loop(0, turns, two_groups, 0)
    arrive(groups - 1)
    build(groups - 1, *odd[:2])

    multiply_side(1 - core, *even)
    multiply_side(1 - core, *odd)
    collect(1 - core)
    sum_copy = remote(
        fields.at[1 - core], from_sibling, sum_send_sems.at[0], sum_recv_sems.at[0], t, sibling
    )
    sum_copy.start()
    multiply_side(core, *even)
    multiply_side(core, *odd)
    collect(core)

    strain, speed, fric = first_state()
    speed = new_speed(0, strain, speed, fric)
    stage(2, speed, speed)
    swaps = row_copies(2) + col_copies(2)
    start(swaps)

    def misfit(sums, speed):
        return speed[0] * (sums[0] * speed[0] - sums[1]) + speed[1] * (
            sums[0] * speed[1] - sums[2]
        )

    sum_copy.wait()
    sums = [fields[core, k] + from_sibling[k] for k in range(CHANNELS)]
    for k in range(CHANNELS):
        chip_sum[k] = sums[k]
    along_send[...] = misfit(sums, speed)
    along_copy = remote(
        along_send, along_recv, sum_send_sems.at[1], sum_recv_sems.at[1], t, partner
    )
    along_copy.start()
    chip_copy = remote(chip_sum, other_sum, sum_send_sems.at[2], sum_recv_sems.at[2], t, partner)
    chip_copy.start()
    wait(swaps)
    strain = strains(speed, 2, (col_halo(2, 0), col_halo(2, 1)))
    along_copy.wait()
    coeff = fric_in[...] - 0.2 * fric * (along_send[...] + along_recv[...])

    fric = drag(coeff)
    send_part(1, strain, speed, fric)
    speed = new_speed(1, strain, speed, fric)
    velocity_out[0, :, columns] = speed[0]
    velocity_out[1, :, columns] = speed[1]
    finals = [
        remote(out, out, out_send_sems.at[k], out_recv_sems.at[k], t, sibling)
        for k, out in enumerate(
            (velocity_out.at[:, :, columns], friction_out.at[:, columns])
        )
    ]
    finals[0].start()
    chip_copy.wait()
    sums = [chip_sum[k] + other_sum[k] for k in range(CHANNELS)]
    friction_out[:, columns] = coeff - 0.2 * fric * misfit(sums, speed)
    finals[1].start()
    wait(finals)

    blocks = packed.at[pl.ds(1, n_tile - 1)]
    pltpu.make_async_copy(blocks, blocks, obs_send_sem).wait()


def body(
    velocity,
    friction,
    thickness,
    rate,
    driving,
    ice_mask,
    obs_velocity,
    obs_weight,
    obs_cells,
    obs_counts,
):
    n_tile, n_layer = lax.axis_size("tile"), lax.axis_size("layer")
    rows, width = friction.shape
    half, quarter = width // 2, width // n_layer
    slots = obs_weight.shape[-1]
    depth = rate.shape[0]
    sides = (4, n_tile // 8, 2) if n_tile % 8 == 0 else (1, n_tile, 1)
    marks = rows * n_layer
    groups = sides[1]
    chunk = (n_tile // groups) * slots
    in_hbm = pl.BlockSpec(memory_space=pltpu.HBM)
    f32 = jnp.float32
    friction_out, velocity_out = pl.pallas_call(
        functools.partial(kernel, sides, n_layer),
        out_shape=(
            pltpu.VMEM(friction.shape, f32),
            pltpu.VMEM(velocity.shape, f32),
        ),
        in_specs=[in_hbm] * 10,
        out_specs=[pl.BlockSpec(memory_space=pltpu.VMEM)] * 2,
        scratch_shapes=[
            pltpu.VMEM((n_tile, 4, slots), f32),
            pltpu.VMEM((n_tile, 4, slots), f32),
            [pltpu.VMEM((CHANNELS * PIECES * marks, chunk), jnp.bfloat16)] * 2,
            [pltpu.VMEM((chunk, quarter), jnp.bfloat16)] * 2,
            [pltpu.VMEM((CHANNELS * PIECES * marks, quarter), f32)] * 2,
            pltpu.VMEM((2, CHANNELS, rows, half), f32),
            pltpu.VMEM((CHANNELS, rows, half), f32),
            pltpu.VMEM((CHANNELS, rows, half), f32),
            pltpu.VMEM((CHANNELS, rows, half), f32),
            pltpu.VMEM((rows, half), f32),
            pltpu.VMEM((rows, half), f32),
            pltpu.VMEM((2 * depth, rows, half), f32),
            pltpu.VMEM((2, rows, half), f32),
            pltpu.VMEM((2, rows, LANES), f32),
            pltpu.VMEM((rows, half), f32),
            pltpu.VMEM((rows, half), f32),
            pltpu.VMEM((2, rows, half), f32),
            pltpu.VMEM((rows, half), jnp.int32),
            pltpu.VMEM((2, rows, half), f32),
            pltpu.VMEM((2, rows, half), f32),
            pltpu.VMEM((4, 2, 2, half), f32),
            pltpu.VMEM((4, 2, 2, 2, half), f32),
            pltpu.VMEM((3, 2, rows, LANES), f32),
            pltpu.VMEM((3, 2, 2, rows, LANES), f32),
            pltpu.VMEM((n_tile, 2 * slots), f32),
            pltpu.VMEM((n_tile, slots), f32),
            pltpu.VMEM((n_tile, slots), jnp.int32),
            pltpu.VMEM((1, n_tile), jnp.int32),
            pltpu.SemaphoreType.DMA((11,)),
            pltpu.SemaphoreType.DMA,
            pltpu.SemaphoreType.DMA((groups,)),
            pltpu.SemaphoreType.DMA((2,)),
            pltpu.SemaphoreType.DMA((2,)),
            pltpu.SemaphoreType.DMA((2,)),
            pltpu.SemaphoreType.DMA((4, 2, 2)),
            pltpu.SemaphoreType.DMA((4, 2, 2)),
            pltpu.SemaphoreType.DMA((3, 2)),
            pltpu.SemaphoreType.DMA((3, 2)),
            pltpu.SemaphoreType.DMA((3,)),
            pltpu.SemaphoreType.DMA((3,)),
            pltpu.SemaphoreType.DMA((2,)),
            pltpu.SemaphoreType.DMA((2,)),
        ],
        compiler_params=pltpu.CompilerParams(
            collective_id=0, has_side_effects=True, vmem_limit_bytes=VMEM_BYTES
        ),
    )(
        velocity,
        friction,
        thickness,
        rate,
        driving,
        ice_mask,
        obs_velocity.reshape(n_tile, 2 * slots),
        obs_weight.reshape(n_tile, slots),
        obs_cells.reshape(n_tile, slots),
        obs_counts.reshape(1, n_tile),
    )
    return friction_out, velocity_out


def solution(mesh):
    placed = (
        P(None, "tile", None),
        P("tile", None),
        P("tile", None),
        P("layer", "tile", None),
        P(None, "tile", None),
        P("tile", None),
        P("tile", "layer", None, None),
        P("tile", "layer", None, None),
        P("tile", "layer", None, None),
        P("tile", "layer", None),
    )
    return jax.shard_map(
        body,
        mesh=mesh,
        in_specs=placed,
        out_specs=(P("tile", None), P(None, "tile", None)),
        check_vma=False,
    )
```

```python
import functools

import jax
import jax.numpy as jnp
from jax import lax
from jax.experimental import pallas as pl
from jax.experimental.pallas import tpu as pltpu
from jax.sharding import PartitionSpec as P

ITERS = 2
MESH = pl.DeviceIdType.MESH
LANES = 128
PIECES = 3
VMEM_BYTES = 58 * 1024 * 1024

CHANNELS = 3


def split_pieces(value):
    pieces = []
    for _ in range(PIECES):
        piece = value.astype(jnp.bfloat16).astype(jnp.float32)
        pieces.append(piece)
        value = value - piece
    return pieces


def kernel(
    sides,
    n_layer,
    velocity,
    friction,
    thickness,
    rate,
    driving,
    ice_mask,
    obs_velocity,
    obs_weight,
    obs_cells,
    obs_counts,
    friction_out,
    velocity_out,
    packed,
    received,
    left_sides,
    right_sides,
    totals,
    fields,
    from_sibling,
    chip_sum,
    other_sum,
    along_send,
    along_recv,
    rates,
    vel,
    edge,
    fric_in,
    thick,
    drive,
    mask,
    part_send,
    part_recv,
    row_send,
    row_recv,
    col_send,
    col_recv,
    seen_in,
    weight_in,
    cells_in,
    counts_in,
    load_sems,
    obs_send_sem,
    obs_recv_sems,
    rate_sems,
    part_send_sems,
    part_recv_sems,
    row_send_sems,
    row_recv_sems,
    col_send_sems,
    col_recv_sems,
    sum_send_sems,
    sum_recv_sems,
    out_send_sems,
    out_recv_sems,
):
    n_x, groups, n_y = sides
    per_group = n_x * n_y
    n_tile = groups * per_group
    t = lax.axis_index("tile")
    l = lax.axis_index("layer")
    rows, width = friction.shape
    half = width // 2
    quarter = width // n_layer
    depth = rate.shape[0]
    total_layers = depth * n_layer
    slots = obs_weight.shape[-1]
    marks = rows * n_layer
    side_marks = CHANNELS * PIECES * marks // 2
    core = lax.rem(l, 2)
    chip = l // 2
    sibling = chip * 2 + (1 - core)
    partner = (1 - chip) * 2 + core
    across = (1 - chip) * 2 + (1 - core)
    above = lax.rem(t + n_tile - 1, n_tile)
    below = lax.rem(t + 1, n_tile)
    first = pl.multiple_of(core * half, LANES)
    columns = pl.ds(first, half)
    sibling_columns = pl.ds(pl.multiple_of((1 - core) * half, LANES), half)

    def remote(src, dst, send_sem, recv_sem, tile, layer):
        return pltpu.make_async_remote_copy(
            src_ref=src,
            dst_ref=dst,
            send_sem=send_sem,
            recv_sem=recv_sem,
            device_id=(tile, layer),
            device_id_type=MESH,
        )

    beside = pl.multiple_of(half - LANES * core, LANES)
    loads = [
        pltpu.make_async_copy(obs_velocity, seen_in, load_sems.at[0]),
        pltpu.make_async_copy(obs_weight, weight_in, load_sems.at[1]),
        pltpu.make_async_copy(obs_cells, cells_in, load_sems.at[2]),
        pltpu.make_async_copy(obs_counts, counts_in, load_sems.at[3]),
        pltpu.make_async_copy(velocity.at[:, :, columns], vel, load_sems.at[4]),
        pltpu.make_async_copy(velocity.at[:, :, pl.ds(beside, LANES)], edge, load_sems.at[5]),
        pltpu.make_async_copy(friction.at[:, columns], fric_in, load_sems.at[6]),
        pltpu.make_async_copy(thickness.at[:, columns], thick, load_sems.at[7]),
        pltpu.make_async_copy(driving.at[:, :, columns], drive, load_sems.at[8]),
        pltpu.make_async_copy(ice_mask.at[:, columns], mask, load_sems.at[9]),
        pltpu.make_async_copy(
            rate.at[:, :, columns], rates.at[pl.ds(core * depth, depth)], load_sems.at[10]
        ),
    ]
    barrier = pltpu.get_barrier_semaphore()
    x, z, y = t // (groups * n_y), lax.rem(t // n_y, groups), lax.rem(t, n_y)

    along_x = [lax.rem(x + k, n_x) * (groups * n_y) for k in range(n_x)]
    along_y = [lax.rem(y + k, n_y) for k in range(n_y)]

    def ring_of(ring):
        odd_ring = lax.rem(ring, 2)
        hop = odd_ring * ((ring + 1) // 2) + (1 - odd_ring) * (groups - ring // 2)
        to_z = lax.rem(z + hop, groups) * n_y
        return [to_x + to_z + to_y for to_x in along_x for to_y in along_y]

    def greet_one(tile, layer):
        pl.semaphore_signal(barrier, inc=1, device_id=(tile, layer), device_id_type=MESH)

    def greet(turn, carry):
        for tile in ring_of(groups - turn):
            greet_one(tile, l)
        return carry

    lax.fori_loop(1, groups, greet, 0)
    for tile in ring_of(0)[1:]:
        greet_one(tile, l)
    greet_one(above, partner)
    greet_one(below, partner)
    for layer in (partner, across, sibling):
        greet_one(t, layer)

    for load in loads:
        load.start()

    for load in loads[:4]:
        load.wait()
    row_id = lax.broadcasted_iota(jnp.int32, (n_tile, n_tile), 0)
    col_id = lax.broadcasted_iota(jnp.int32, (n_tile, n_tile), 1)
    counts = jnp.sum(
        jnp.where(row_id == col_id, counts_in[...].astype(jnp.float32), 0.0), axis=1, keepdims=True
    )
    place = lax.broadcasted_iota(jnp.int32, (n_tile, slots), 1).astype(jnp.float32)
    weight = jnp.where(place < counts, weight_in[...], 0.0)
    packed[:, 0, :] = weight
    packed[:, 1, :] = weight * seen_in[:, :slots]
    packed[:, 2, :] = weight * seen_in[:, slots:]
    packed[:, 3, :] = cells_in[...].astype(jnp.float32)

    for load in loads[4:6]:
        load.wait()
    row_send[0, 0] = vel[:, 0, :]
    row_send[0, 1] = vel[:, rows - 1, :]

    pl.semaphore_wait(barrier, n_tile - 1 + 2 + n_layer - 1)

    def row_copies(phase):
        copies = []
        for side, tile in ((0, above), (1, below)):
            for source, layer in enumerate((l, partner) if phase % 2 else (l,)):
                copies.append(
                    remote(
                        row_send.at[phase, side],
                        row_recv.at[phase, 1 - side, source],
                        row_send_sems.at[phase, side, source],
                        row_recv_sems.at[phase, 1 - side, source],
                        tile,
                        layer,
                    )
                )
        return copies

    def col_copies(phase):
        return [
            remote(
                col_send.at[phase - 1],
                col_recv.at[phase - 1, source],
                col_send_sems.at[phase - 1, source],
                col_recv_sems.at[phase - 1, source],
                t,
                layer,
            )
            for source, layer in enumerate((sibling, across) if phase % 2 else (sibling,))
        ]

    def part_copy(turn):
        return remote(
            part_send.at[turn],
            part_recv.at[turn],
            part_send_sems.at[turn],
            part_recv_sems.at[turn],
            t,
            partner,
        )

    def start(copies):
        for copy in copies:
            copy.start()

    def wait(copies):
        for copy in copies:
            copy.wait()

    start(row_copies(0))
    own_block = pltpu.make_async_copy(packed.at[t], received.at[0], obs_recv_sems.at[0])
    own_block.start()

    def send_obs(tile, ring, k):
        remote(
            packed.at[tile],
            received.at[ring * per_group + k],
            obs_send_sem,
            obs_recv_sems.at[ring],
            tile,
            l,
        ).start()

    def send_ring(ring, carry):
        for k, tile in enumerate(ring_of(ring)):
            send_obs(tile, ring, k)
        return carry

    for k, tile in enumerate(ring_of(0)):
        if k > 0:
            send_obs(tile, 0, k)
    lax.fori_loop(1, groups, send_ring, 0)
    rate_copy = remote(
        rate.at[:, :, sibling_columns],
        rates.at[pl.ds(core * depth, depth)],
        rate_sems.at[0],
        rate_sems.at[1],
        t,
        sibling,
    )
    rate_copy.start()

    row_of = lax.broadcasted_iota(jnp.int32, (rows, half), 0)
    col_of = lax.broadcasted_iota(jnp.int32, (rows, half), 1)
    top, bottom = t == 0, t == n_tile - 1
    at_left = core == 0

    def diff_rows(field, low, high):
        low = jnp.where(top, 0.0, low)
        high = jnp.where(bottom, 0.0, high)
        previous = jnp.where(row_of == 0, low, pltpu.roll(field, 1, 0))
        following = jnp.where(row_of == rows - 1, high, pltpu.roll(field, rows - 1, 0))
        return 0.5 * (following - previous)

    def diff_cols(field, tile):
        low = jnp.where(at_left, 0.0, tile[:, LANES - 1 : LANES])
        high = jnp.where(at_left, tile[:, 0:1], 0.0)
        previous = jnp.where(col_of == 0, low, pltpu.roll(field, 1, 1))
        following = jnp.where(col_of == half - 1, high, pltpu.roll(field, half - 1, 1))
        return 0.5 * (following - previous)

    def row_halo(phase, k):
        low, high = row_recv[phase, 0, 0, k : k + 1, :], row_recv[phase, 1, 0, k : k + 1, :]
        if phase % 2:
            low = low + row_recv[phase, 0, 1, k : k + 1, :]
            high = high + row_recv[phase, 1, 1, k : k + 1, :]
        return low, high

    def col_halo(phase, k):
        tile = col_recv[phase - 1, 0, k]
        return tile + col_recv[phase - 1, 1, k] if phase % 2 else tile

    def stage(phase, by_row, by_col):
        for k in range(2):
            row_send[phase, 0, k : k + 1, :] = by_row[k][0:1, :]
            row_send[phase, 1, k : k + 1, :] = by_row[k][rows - 1 : rows, :]
            col_send[phase - 1, k] = jnp.where(
                at_left, by_col[k][:, half - LANES :], by_col[k][:, :LANES]
            )

    def strains(speed, phase, tiles):
        exx = diff_rows(speed[0], *row_halo(phase, 0))
        eyy = diff_cols(speed[1], tiles[1])
        exy = 0.5 * (diff_cols(speed[0], tiles[0]) + diff_rows(speed[1], *row_halo(phase, 1)))
        return exx, eyy, exy

    def stresses(strain, visc):
        exx, eyy, exy = strain
        return 2.0 * visc * (2.0 * exx + eyy), 2.0 * visc * (2.0 * eyy + exx), 2.0 * visc * exy

    chip_layers = 2 * depth
    first_layer = (chip * chip_layers).astype(jnp.float32)

    def make_part(turn, strain, speed, fric):
        exx, eyy, exy = strain
        e2 = exx * exx + eyy * eyy + exx * eyy + exy * exy + 0.05
        b2 = 0.25 * fric * fric * (speed[0] * speed[0] + speed[1] * speed[1])
        layer_sum = jnp.zeros_like(e2)
        for k in range(chip_layers):
            height = 1.0 - (first_layer + (k + 0.5)) * (1.0 / total_layers)
            layer_sum = layer_sum + rates[k] * jnp.exp(
                jnp.log(e2 + (height * height) * b2) * (-1.0 / 3.0)
            )
        part = thick[...] * (layer_sum * (1.0 / total_layers))
        part_send[turn] = part
        sxx, syy, sxy = stresses(strain, part)
        phase = 2 * turn + 1
        stage(phase, (sxx, sxy), (sxy, syy))

    def send_part(turn):
        phase = 2 * turn + 1
        start(row_copies(phase))
        part_copy(turn).start()
        start(col_copies(phase))

    def new_speed(turn, strain, speed, fric):
        phase = 2 * turn + 1
        wait(row_copies(phase) + [part_copy(turn)] + col_copies(phase))
        visc = part_send[turn] + part_recv[turn]
        sxx, syy, sxy = stresses(strain, visc)
        div_0 = diff_rows(sxx, *row_halo(phase, 0)) + diff_cols(sxy, col_halo(phase, 0))
        div_1 = diff_rows(sxy, *row_halo(phase, 1)) + diff_cols(syy, col_halo(phase, 1))
        icy = jnp.where(mask[...] >= 1, 1.0, 0.0)
        scale = 0.5 * icy / (1.0 + fric + 4.0 * visc)
        return (
            speed[0] + scale * (div_0 - fric * speed[0] + drive[0]),
            speed[1] + scale * (div_1 - fric * speed[1] + drive[1]),
        )

    def drag(coeff):
        return jnp.where(mask[...] == 2, 1.0, 0.0) * jnp.exp(coeff)

    def first_state():
        speed = (vel[0], vel[1])
        return strains(speed, 0, (edge[0], edge[1])), speed, drag(fric_in[...])

    for total in totals:
        total[...] = jnp.zeros_like(total)
    mark_id = lax.broadcasted_iota(jnp.int32, (marks, slots), 0).astype(jnp.float32)
    lane_id = lax.broadcasted_iota(jnp.int32, (slots, quarter), 1).astype(jnp.float32)

    def arrive(group):
        blocks = received.at[pl.ds(group * per_group, per_group)]
        pltpu.make_async_copy(blocks, blocks, obs_recv_sems.at[group]).wait()

    def build(group, left_side, right_side):
        block = received[pl.ds(group * per_group, per_group)]
        cell = block[:, 3, :]
        mark = jnp.floor((cell + 0.5) * (1.0 / quarter))
        column = cell - mark * quarter
        row = jnp.floor((mark + 0.5) * (1.0 / n_layer))
        mark = (mark - row * n_layer) * rows + row
        column = column.T
        pieces = []
        for channel in range(CHANNELS):
            pieces += split_pieces(block[:, channel, :])
        for b in range(per_group):
            hit = mark[b : b + 1, :] == mark_id
            for p, piece in enumerate(pieces):
                marked = jnp.where(hit, piece[b : b + 1, :], 0.0).astype(jnp.bfloat16)
                for side in range(2):
                    at = side * side_marks + p * (marks // 2)
                    left_side[at : at + marks // 2, b * slots : (b + 1) * slots] = marked[
                        side * (marks // 2) : (side + 1) * (marks // 2)
                    ]
            right_side[b * slots : (b + 1) * slots, :] = jnp.where(
                column[:, b : b + 1] == lane_id, 1.0, 0.0
            ).astype(jnp.bfloat16)

    def multiply(left_side, right_side, total):
        total[...] += jnp.dot(left_side[...], right_side[...], preferred_element_type=jnp.float32)

    def multiply_side(side, left_side, right_side, total):
        part = pl.ds(pl.multiple_of(side * side_marks, side_marks), side_marks)
        total[part, :] += jnp.dot(
            left_side[part, :], right_side[...], preferred_element_type=jnp.float32
        )

    even = (left_sides[0], right_sides[0], totals[0])
    odd = (left_sides[1], right_sides[1], totals[1])
    turns = groups // 2 - 1

    def two_groups(turn, carry):
        arrive(2 * turn + 1)
        arrive(2 * turn + 2)
        build(2 * turn + 1, *odd[:2])
        multiply(*even)
        build(2 * turn + 2, *even[:2])
        multiply(*odd)
        return carry

    def collect(side):
        for channel in range(CHANNELS):
            for q in range(2):
                field = None
                for piece in range(PIECES):
                    at = side * side_marks + ((channel * PIECES + piece) * 2 + q) * rows
                    part = pl.ds(pl.multiple_of(at, rows), rows)
                    value = totals[0][part, :] + totals[1][part, :]
                    field = value if field is None else field + value
                fields[side, channel, :, q * quarter : (q + 1) * quarter] = field

    arrive(0)
    build(0, *even[:2])

    arrive(1)
    arrive(2)
    wait(loads[6:])
    rate_copy.wait()
    wait(row_copies(0))
    build(1, *odd[:2])
    strain, speed, fric = first_state()
    make_part(0, strain, speed, fric)
    multiply(*even)
    build(2, *even[:2])
    multiply(*odd)
    send_part(0)

    lax.fori_loop(1, turns, two_groups, 0)
    arrive(groups - 1)
    build(groups - 1, *odd[:2])

    multiply_side(1 - core, *even)
    multiply_side(1 - core, *odd)
    collect(1 - core)
    sum_copy = remote(
        fields.at[1 - core], from_sibling, sum_send_sems.at[0], sum_recv_sems.at[0], t, sibling
    )
    sum_copy.start()

    strain, speed, fric = first_state()
    speed = new_speed(0, strain, speed, fric)
    stage(2, speed, speed)
    multiply_side(core, *even)
    multiply_side(core, *odd)
    collect(core)
    swaps = row_copies(2) + col_copies(2)
    start(swaps)

    def misfit(sums, speed):
        return speed[0] * (sums[0] * speed[0] - sums[1]) + speed[1] * (
            sums[0] * speed[1] - sums[2]
        )

    sum_copy.wait()
    sums = [fields[core, k] + from_sibling[k] for k in range(CHANNELS)]
    for k in range(CHANNELS):
        chip_sum[k] = sums[k]
    along_send[...] = misfit(sums, speed)
    along_copy = remote(
        along_send, along_recv, sum_send_sems.at[1], sum_recv_sems.at[1], t, partner
    )
    along_copy.start()
    chip_copy = remote(chip_sum, other_sum, sum_send_sems.at[2], sum_recv_sems.at[2], t, partner)
    chip_copy.start()
    wait(swaps)
    strain = strains(speed, 2, (col_halo(2, 0), col_halo(2, 1)))
    along_copy.wait()
    coeff = fric_in[...] - 0.2 * fric * (along_send[...] + along_recv[...])

    fric = drag(coeff)
    make_part(1, strain, speed, fric)
    send_part(1)
    speed = new_speed(1, strain, speed, fric)
    velocity_out[0, :, columns] = speed[0]
    velocity_out[1, :, columns] = speed[1]
    finals = [
        remote(out, out, out_send_sems.at[k], out_recv_sems.at[k], t, sibling)
        for k, out in enumerate(
            (velocity_out.at[:, :, columns], friction_out.at[:, columns])
        )
    ]
    finals[0].start()
    chip_copy.wait()
    sums = [chip_sum[k] + other_sum[k] for k in range(CHANNELS)]
    friction_out[:, columns] = coeff - 0.2 * fric * misfit(sums, speed)
    finals[1].start()
    wait(finals)

    blocks = packed.at[pl.ds(1, n_tile - 1)]
    pltpu.make_async_copy(blocks, blocks, obs_send_sem).wait()


def body(
    velocity,
    friction,
    thickness,
    rate,
    driving,
    ice_mask,
    obs_velocity,
    obs_weight,
    obs_cells,
    obs_counts,
):
    n_tile, n_layer = lax.axis_size("tile"), lax.axis_size("layer")
    rows, width = friction.shape
    half, quarter = width // 2, width // n_layer
    slots = obs_weight.shape[-1]
    depth = rate.shape[0]
    sides = (4, n_tile // 8, 2) if n_tile % 8 == 0 else (1, n_tile, 1)
    marks = rows * n_layer
    groups = sides[1]
    chunk = (n_tile // groups) * slots
    in_hbm = pl.BlockSpec(memory_space=pltpu.HBM)
    f32 = jnp.float32
    friction_out, velocity_out = pl.pallas_call(
        functools.partial(kernel, sides, n_layer),
        out_shape=(
            pltpu.VMEM(friction.shape, f32),
            pltpu.VMEM(velocity.shape, f32),
        ),
        in_specs=[in_hbm] * 10,
        out_specs=[pl.BlockSpec(memory_space=pltpu.VMEM)] * 2,
        scratch_shapes=[
            pltpu.VMEM((n_tile, 4, slots), f32),
            pltpu.VMEM((n_tile, 4, slots), f32),
            [pltpu.VMEM((CHANNELS * PIECES * marks, chunk), jnp.bfloat16)] * 2,
            [pltpu.VMEM((chunk, quarter), jnp.bfloat16)] * 2,
            [pltpu.VMEM((CHANNELS * PIECES * marks, quarter), f32)] * 2,
            pltpu.VMEM((2, CHANNELS, rows, half), f32),
            pltpu.VMEM((CHANNELS, rows, half), f32),
            pltpu.VMEM((CHANNELS, rows, half), f32),
            pltpu.VMEM((CHANNELS, rows, half), f32),
            pltpu.VMEM((rows, half), f32),
            pltpu.VMEM((rows, half), f32),
            pltpu.VMEM((2 * depth, rows, half), f32),
            pltpu.VMEM((2, rows, half), f32),
            pltpu.VMEM((2, rows, LANES), f32),
            pltpu.VMEM((rows, half), f32),
            pltpu.VMEM((rows, half), f32),
            pltpu.VMEM((2, rows, half), f32),
            pltpu.VMEM((rows, half), jnp.int32),
            pltpu.VMEM((2, rows, half), f32),
            pltpu.VMEM((2, rows, half), f32),
            pltpu.VMEM((4, 2, 2, half), f32),
            pltpu.VMEM((4, 2, 2, 2, half), f32),
            pltpu.VMEM((3, 2, rows, LANES), f32),
            pltpu.VMEM((3, 2, 2, rows, LANES), f32),
            pltpu.VMEM((n_tile, 2 * slots), f32),
            pltpu.VMEM((n_tile, slots), f32),
            pltpu.VMEM((n_tile, slots), jnp.int32),
            pltpu.VMEM((1, n_tile), jnp.int32),
            pltpu.SemaphoreType.DMA((11,)),
            pltpu.SemaphoreType.DMA,
            pltpu.SemaphoreType.DMA((groups,)),
            pltpu.SemaphoreType.DMA((2,)),
            pltpu.SemaphoreType.DMA((2,)),
            pltpu.SemaphoreType.DMA((2,)),
            pltpu.SemaphoreType.DMA((4, 2, 2)),
            pltpu.SemaphoreType.DMA((4, 2, 2)),
            pltpu.SemaphoreType.DMA((3, 2)),
            pltpu.SemaphoreType.DMA((3, 2)),
            pltpu.SemaphoreType.DMA((3,)),
            pltpu.SemaphoreType.DMA((3,)),
            pltpu.SemaphoreType.DMA((2,)),
            pltpu.SemaphoreType.DMA((2,)),
        ],
        compiler_params=pltpu.CompilerParams(
            collective_id=0, has_side_effects=True, vmem_limit_bytes=VMEM_BYTES
        ),
    )(
        velocity,
        friction,
        thickness,
        rate,
        driving,
        ice_mask,
        obs_velocity.reshape(n_tile, 2 * slots),
        obs_weight.reshape(n_tile, slots),
        obs_cells.reshape(n_tile, slots),
        obs_counts.reshape(1, n_tile),
    )
    return friction_out, velocity_out


def solution(mesh):
    placed = (
        P(None, "tile", None),
        P("tile", None),
        P("tile", None),
        P("layer", "tile", None),
        P(None, "tile", None),
        P("tile", None),
        P("tile", "layer", None, None),
        P("tile", "layer", None, None),
        P("tile", "layer", None, None),
        P("tile", "layer", None),
    )
    return jax.shard_map(
        body,
        mesh=mesh,
        in_specs=placed,
        out_specs=(P("tile", None), P(None, "tile", None)),
        check_vma=False,
    )
```

```python
import functools

import jax
import jax.numpy as jnp
from jax import lax
from jax.experimental import pallas as pl
from jax.experimental.pallas import tpu as pltpu
from jax.sharding import PartitionSpec as P

ITERS = 2
MESH = pl.DeviceIdType.MESH
LANES = 128
PIECES = 3
VMEM_BYTES = 58 * 1024 * 1024

CHANNELS = 3


def split_pieces(value):
    pieces = []
    for _ in range(PIECES):
        piece = value.astype(jnp.bfloat16).astype(jnp.float32)
        pieces.append(piece)
        value = value - piece
    return pieces


def kernel(
    sides,
    n_layer,
    velocity,
    friction,
    thickness,
    rate,
    driving,
    ice_mask,
    obs_velocity,
    obs_weight,
    obs_cells,
    obs_counts,
    friction_out,
    velocity_out,
    packed,
    received,
    left_sides,
    right_sides,
    totals,
    fields,
    from_sibling,
    chip_sum,
    other_sum,
    along_send,
    along_recv,
    rates,
    vel,
    edge,
    fric_in,
    thick,
    drive,
    mask,
    part_send,
    part_recv,
    row_send,
    row_recv,
    col_send,
    col_recv,
    seen_in,
    weight_in,
    cells_in,
    counts_in,
    load_sems,
    obs_send_sem,
    obs_recv_sems,
    rate_sems,
    part_send_sems,
    part_recv_sems,
    row_send_sems,
    row_recv_sems,
    col_send_sems,
    col_recv_sems,
    sum_send_sems,
    sum_recv_sems,
    out_send_sems,
    out_recv_sems,
):
    n_x, groups, n_y = sides
    per_group = n_x * n_y
    n_tile = groups * per_group
    t = lax.axis_index("tile")
    l = lax.axis_index("layer")
    rows, width = friction.shape
    half = width // 2
    quarter = width // n_layer
    depth = rate.shape[0]
    total_layers = depth * n_layer
    slots = obs_weight.shape[-1]
    marks = rows * n_layer
    side_marks = CHANNELS * PIECES * marks // 2
    core = lax.rem(l, 2)
    chip = l // 2
    sibling = chip * 2 + (1 - core)
    partner = (1 - chip) * 2 + core
    across = (1 - chip) * 2 + (1 - core)
    above = lax.rem(t + n_tile - 1, n_tile)
    below = lax.rem(t + 1, n_tile)
    first = pl.multiple_of(core * half, LANES)
    columns = pl.ds(first, half)
    sibling_columns = pl.ds(pl.multiple_of((1 - core) * half, LANES), half)

    def remote(src, dst, send_sem, recv_sem, tile, layer):
        return pltpu.make_async_remote_copy(
            src_ref=src,
            dst_ref=dst,
            send_sem=send_sem,
            recv_sem=recv_sem,
            device_id=(tile, layer),
            device_id_type=MESH,
        )

    beside = pl.multiple_of(half - LANES * core, LANES)
    loads = [
        pltpu.make_async_copy(obs_velocity, seen_in, load_sems.at[0]),
        pltpu.make_async_copy(obs_weight, weight_in, load_sems.at[1]),
        pltpu.make_async_copy(obs_cells, cells_in, load_sems.at[2]),
        pltpu.make_async_copy(obs_counts, counts_in, load_sems.at[3]),
        pltpu.make_async_copy(velocity.at[:, :, columns], vel, load_sems.at[4]),
        pltpu.make_async_copy(velocity.at[:, :, pl.ds(beside, LANES)], edge, load_sems.at[5]),
        pltpu.make_async_copy(friction.at[:, columns], fric_in, load_sems.at[6]),
        pltpu.make_async_copy(thickness.at[:, columns], thick, load_sems.at[7]),
        pltpu.make_async_copy(driving.at[:, :, columns], drive, load_sems.at[8]),
        pltpu.make_async_copy(ice_mask.at[:, columns], mask, load_sems.at[9]),
        pltpu.make_async_copy(
            rate.at[:, :, columns], rates.at[pl.ds(core * depth, depth)], load_sems.at[10]
        ),
    ]
    barrier = pltpu.get_barrier_semaphore()
    x, z, y = t // (groups * n_y), lax.rem(t // n_y, groups), lax.rem(t, n_y)

    along_x = [lax.rem(x + k, n_x) * (groups * n_y) for k in range(n_x)]
    along_y = [lax.rem(y + k, n_y) for k in range(n_y)]

    def ring_of(ring):
        odd_ring = lax.rem(ring, 2)
        hop = odd_ring * ((ring + 1) // 2) + (1 - odd_ring) * (groups - ring // 2)
        to_z = lax.rem(z + hop, groups) * n_y
        return [to_x + to_z + to_y for to_x in along_x for to_y in along_y]

    def greet_one(tile, layer):
        pl.semaphore_signal(barrier, inc=1, device_id=(tile, layer), device_id_type=MESH)

    def greet(turn, carry):
        for tile in ring_of(groups - turn):
            greet_one(tile, l)
        return carry

    lax.fori_loop(1, groups, greet, 0)
    for tile in ring_of(0)[1:]:
        greet_one(tile, l)
    greet_one(above, partner)
    greet_one(below, partner)
    for layer in (partner, across, sibling):
        greet_one(t, layer)

    for load in loads:
        load.start()

    for load in loads[:4]:
        load.wait()
    row_id = lax.broadcasted_iota(jnp.int32, (n_tile, n_tile), 0)
    col_id = lax.broadcasted_iota(jnp.int32, (n_tile, n_tile), 1)
    counts = jnp.sum(
        jnp.where(row_id == col_id, counts_in[...].astype(jnp.float32), 0.0), axis=1, keepdims=True
    )
    place = lax.broadcasted_iota(jnp.int32, (n_tile, slots), 1).astype(jnp.float32)
    weight = jnp.where(place < counts, weight_in[...], 0.0)
    packed[:, 0, :] = weight
    packed[:, 1, :] = weight * seen_in[:, :slots]
    packed[:, 2, :] = weight * seen_in[:, slots:]
    packed[:, 3, :] = cells_in[...].astype(jnp.float32)

    for load in loads[4:6]:
        load.wait()
    row_send[0, 0] = vel[:, 0, :]
    row_send[0, 1] = vel[:, rows - 1, :]

    pl.semaphore_wait(barrier, n_tile - 1 + 2 + n_layer - 1)

    def row_copies(phase):
        copies = []
        for side, tile in ((0, above), (1, below)):
            for source, layer in enumerate((l, partner) if phase % 2 else (l,)):
                copies.append(
                    remote(
                        row_send.at[phase, side],
                        row_recv.at[phase, 1 - side, source],
                        row_send_sems.at[phase, side, source],
                        row_recv_sems.at[phase, 1 - side, source],
                        tile,
                        layer,
                    )
                )
        return copies

    def col_copies(phase):
        return [
            remote(
                col_send.at[phase - 1],
                col_recv.at[phase - 1, source],
                col_send_sems.at[phase - 1, source],
                col_recv_sems.at[phase - 1, source],
                t,
                layer,
            )
            for source, layer in enumerate((sibling, across) if phase % 2 else (sibling,))
        ]

    def part_copy(turn):
        return remote(
            part_send.at[turn],
            part_recv.at[turn],
            part_send_sems.at[turn],
            part_recv_sems.at[turn],
            t,
            partner,
        )

    def start(copies):
        for copy in copies:
            copy.start()

    def wait(copies):
        for copy in copies:
            copy.wait()

    start(row_copies(0))
    own_block = pltpu.make_async_copy(packed.at[t], received.at[0], obs_recv_sems.at[0])
    own_block.start()

    def send_obs(tile, ring, k):
        remote(
            packed.at[tile],
            received.at[ring * per_group + k],
            obs_send_sem,
            obs_recv_sems.at[ring],
            tile,
            l,
        ).start()

    def send_ring(ring, carry):
        for k, tile in enumerate(ring_of(ring)):
            send_obs(tile, ring, k)
        return carry

    for k, tile in enumerate(ring_of(0)):
        if k > 0:
            send_obs(tile, 0, k)
    lax.fori_loop(1, groups, send_ring, 0)
    rate_copy = remote(
        rate.at[:, :, sibling_columns],
        rates.at[pl.ds(core * depth, depth)],
        rate_sems.at[0],
        rate_sems.at[1],
        t,
        sibling,
    )
    rate_copy.start()

    row_of = lax.broadcasted_iota(jnp.int32, (rows, half), 0)
    col_of = lax.broadcasted_iota(jnp.int32, (rows, half), 1)
    top, bottom = t == 0, t == n_tile - 1
    at_left = core == 0

    def diff_rows(field, low, high):
        low = jnp.where(top, 0.0, low)
        high = jnp.where(bottom, 0.0, high)
        previous = jnp.where(row_of == 0, low, pltpu.roll(field, 1, 0))
        following = jnp.where(row_of == rows - 1, high, pltpu.roll(field, rows - 1, 0))
        return 0.5 * (following - previous)

    def diff_cols(field, tile):
        low = jnp.where(at_left, 0.0, tile[:, LANES - 1 : LANES])
        high = jnp.where(at_left, tile[:, 0:1], 0.0)
        previous = jnp.where(col_of == 0, low, pltpu.roll(field, 1, 1))
        following = jnp.where(col_of == half - 1, high, pltpu.roll(field, half - 1, 1))
        return 0.5 * (following - previous)

    def row_halo(phase, k):
        low, high = row_recv[phase, 0, 0, k : k + 1, :], row_recv[phase, 1, 0, k : k + 1, :]
        if phase % 2:
            low = low + row_recv[phase, 0, 1, k : k + 1, :]
            high = high + row_recv[phase, 1, 1, k : k + 1, :]
        return low, high

    def col_halo(phase, k):
        tile = col_recv[phase - 1, 0, k]
        return tile + col_recv[phase - 1, 1, k] if phase % 2 else tile

    def stage(phase, by_row, by_col):
        for k in range(2):
            row_send[phase, 0, k : k + 1, :] = by_row[k][0:1, :]
            row_send[phase, 1, k : k + 1, :] = by_row[k][rows - 1 : rows, :]
            col_send[phase - 1, k] = jnp.where(
                at_left, by_col[k][:, half - LANES :], by_col[k][:, :LANES]
            )

    def strains(speed, phase, tiles):
        exx = diff_rows(speed[0], *row_halo(phase, 0))
        eyy = diff_cols(speed[1], tiles[1])
        exy = 0.5 * (diff_cols(speed[0], tiles[0]) + diff_rows(speed[1], *row_halo(phase, 1)))
        return exx, eyy, exy

    def stresses(strain, visc):
        exx, eyy, exy = strain
        return 2.0 * visc * (2.0 * exx + eyy), 2.0 * visc * (2.0 * eyy + exx), 2.0 * visc * exy

    chip_layers = 2 * depth
    first_layer = (chip * chip_layers).astype(jnp.float32)

    def make_part(turn, strain, speed, fric):
        exx, eyy, exy = strain
        e2 = exx * exx + eyy * eyy + exx * eyy + exy * exy + 0.05
        b2 = 0.25 * fric * fric * (speed[0] * speed[0] + speed[1] * speed[1])
        layer_sum = jnp.zeros_like(e2)
        for k in range(chip_layers):
            height = 1.0 - (first_layer + (k + 0.5)) * (1.0 / total_layers)
            layer_sum = layer_sum + rates[k] * jnp.exp(
                jnp.log(e2 + (height * height) * b2) * (-1.0 / 3.0)
            )
        part = thick[...] * (layer_sum * (1.0 / total_layers))
        part_send[turn] = part
        sxx, syy, sxy = stresses(strain, part)
        phase = 2 * turn + 1
        stage(phase, (sxx, sxy), (sxy, syy))

    def send_part(turn):
        phase = 2 * turn + 1
        start(row_copies(phase))
        part_copy(turn).start()
        start(col_copies(phase))

    def new_speed(turn, strain, speed, fric):
        phase = 2 * turn + 1
        wait(row_copies(phase) + [part_copy(turn)] + col_copies(phase))
        visc = part_send[turn] + part_recv[turn]
        sxx, syy, sxy = stresses(strain, visc)
        div_0 = diff_rows(sxx, *row_halo(phase, 0)) + diff_cols(sxy, col_halo(phase, 0))
        div_1 = diff_rows(sxy, *row_halo(phase, 1)) + diff_cols(syy, col_halo(phase, 1))
        icy = jnp.where(mask[...] >= 1, 1.0, 0.0)
        scale = 0.5 * icy / (1.0 + fric + 4.0 * visc)
        return (
            speed[0] + scale * (div_0 - fric * speed[0] + drive[0]),
            speed[1] + scale * (div_1 - fric * speed[1] + drive[1]),
        )

    def drag(coeff):
        return jnp.where(mask[...] == 2, 1.0, 0.0) * jnp.exp(coeff)

    def first_state():
        speed = (vel[0], vel[1])
        return strains(speed, 0, (edge[0], edge[1])), speed, drag(fric_in[...])

    for total in totals:
        total[...] = jnp.zeros_like(total)
    mark_id = lax.broadcasted_iota(jnp.int32, (marks, slots), 0).astype(jnp.float32)
    lane_id = lax.broadcasted_iota(jnp.int32, (slots, quarter), 1).astype(jnp.float32)

    def arrive(group):
        blocks = received.at[pl.ds(group * per_group, per_group)]
        pltpu.make_async_copy(blocks, blocks, obs_recv_sems.at[group]).wait()

    def build(group, left_side, right_side):
        block = received[pl.ds(group * per_group, per_group)]
        cell = block[:, 3, :]
        mark = jnp.floor((cell + 0.5) * (1.0 / quarter))
        column = cell - mark * quarter
        row = jnp.floor((mark + 0.5) * (1.0 / n_layer))
        mark = (mark - row * n_layer) * rows + row
        column = column.T
        pieces = []
        for channel in range(CHANNELS):
            pieces += split_pieces(block[:, channel, :])
        for b in range(per_group):
            hit = mark[b : b + 1, :] == mark_id
            for p, piece in enumerate(pieces):
                marked = jnp.where(hit, piece[b : b + 1, :], 0.0).astype(jnp.bfloat16)
                for side in range(2):
                    at = side * side_marks + p * (marks // 2)
                    left_side[at : at + marks // 2, b * slots : (b + 1) * slots] = marked[
                        side * (marks // 2) : (side + 1) * (marks // 2)
                    ]
            right_side[b * slots : (b + 1) * slots, :] = jnp.where(
                column[:, b : b + 1] == lane_id, 1.0, 0.0
            ).astype(jnp.bfloat16)

    def multiply(left_side, right_side, total):
        total[...] += jnp.dot(left_side[...], right_side[...], preferred_element_type=jnp.float32)

    def multiply_side(side, left_side, right_side, total):
        part = pl.ds(pl.multiple_of(side * side_marks, side_marks), side_marks)
        total[part, :] += jnp.dot(
            left_side[part, :], right_side[...], preferred_element_type=jnp.float32
        )

    even = (left_sides[0], right_sides[0], totals[0])
    odd = (left_sides[1], right_sides[1], totals[1])
    turns = groups // 2 - 1

    def two_groups(turn, carry):
        arrive(2 * turn + 1)
        arrive(2 * turn + 2)
        build(2 * turn + 1, *odd[:2])
        multiply(*even)
        build(2 * turn + 2, *even[:2])
        multiply(*odd)
        return carry

    def collect(side):
        for channel in range(CHANNELS):
            for q in range(2):
                field = None
                for piece in range(PIECES):
                    at = side * side_marks + ((channel * PIECES + piece) * 2 + q) * rows
                    part = pl.ds(pl.multiple_of(at, rows), rows)
                    value = totals[0][part, :] + totals[1][part, :]
                    field = value if field is None else field + value
                fields[side, channel, :, q * quarter : (q + 1) * quarter] = field

    arrive(0)
    build(0, *even[:2])

    arrive(1)
    wait(loads[6:])
    rate_copy.wait()
    wait(row_copies(0))
    build(1, *odd[:2])
    strain, speed, fric = first_state()
    make_part(0, strain, speed, fric)
    multiply(*even)
    arrive(2)
    build(2, *even[:2])
    multiply(*odd)
    send_part(0)

    lax.fori_loop(1, turns, two_groups, 0)
    arrive(groups - 1)
    build(groups - 1, *odd[:2])

    multiply_side(1 - core, *even)
    multiply_side(1 - core, *odd)
    collect(1 - core)
    sum_copy = remote(
        fields.at[1 - core], from_sibling, sum_send_sems.at[0], sum_recv_sems.at[0], t, sibling
    )
    sum_copy.start()

    strain, speed, fric = first_state()
    speed = new_speed(0, strain, speed, fric)
    stage(2, speed, speed)
    multiply_side(core, *even)
    multiply_side(core, *odd)
    collect(core)
    swaps = row_copies(2) + col_copies(2)
    start(swaps)

    def misfit(sums, speed):
        return speed[0] * (sums[0] * speed[0] - sums[1]) + speed[1] * (
            sums[0] * speed[1] - sums[2]
        )

    sum_copy.wait()
    sums = [fields[core, k] + from_sibling[k] for k in range(CHANNELS)]
    for k in range(CHANNELS):
        chip_sum[k] = sums[k]
    along_send[...] = misfit(sums, speed)
    along_copy = remote(
        along_send, along_recv, sum_send_sems.at[1], sum_recv_sems.at[1], t, partner
    )
    along_copy.start()
    chip_copy = remote(chip_sum, other_sum, sum_send_sems.at[2], sum_recv_sems.at[2], t, partner)
    chip_copy.start()
    wait(swaps)
    strain = strains(speed, 2, (col_halo(2, 0), col_halo(2, 1)))
    along_copy.wait()
    coeff = fric_in[...] - 0.2 * fric * (along_send[...] + along_recv[...])

    fric = drag(coeff)
    make_part(1, strain, speed, fric)
    send_part(1)
    speed = new_speed(1, strain, speed, fric)
    velocity_out[0, :, columns] = speed[0]
    velocity_out[1, :, columns] = speed[1]
    finals = [
        remote(out, out, out_send_sems.at[k], out_recv_sems.at[k], t, sibling)
        for k, out in enumerate(
            (velocity_out.at[:, :, columns], friction_out.at[:, columns])
        )
    ]
    finals[0].start()
    chip_copy.wait()
    sums = [chip_sum[k] + other_sum[k] for k in range(CHANNELS)]
    friction_out[:, columns] = coeff - 0.2 * fric * misfit(sums, speed)
    finals[1].start()
    wait(finals)

    blocks = packed.at[pl.ds(1, n_tile - 1)]
    pltpu.make_async_copy(blocks, blocks, obs_send_sem).wait()


def body(
    velocity,
    friction,
    thickness,
    rate,
    driving,
    ice_mask,
    obs_velocity,
    obs_weight,
    obs_cells,
    obs_counts,
):
    n_tile, n_layer = lax.axis_size("tile"), lax.axis_size("layer")
    rows, width = friction.shape
    half, quarter = width // 2, width // n_layer
    slots = obs_weight.shape[-1]
    depth = rate.shape[0]
    sides = (4, n_tile // 8, 2) if n_tile % 8 == 0 else (1, n_tile, 1)
    marks = rows * n_layer
    groups = sides[1]
    chunk = (n_tile // groups) * slots
    in_hbm = pl.BlockSpec(memory_space=pltpu.HBM)
    f32 = jnp.float32
    friction_out, velocity_out = pl.pallas_call(
        functools.partial(kernel, sides, n_layer),
        out_shape=(
            pltpu.VMEM(friction.shape, f32),
            pltpu.VMEM(velocity.shape, f32),
        ),
        in_specs=[in_hbm] * 10,
        out_specs=[pl.BlockSpec(memory_space=pltpu.VMEM)] * 2,
        scratch_shapes=[
            pltpu.VMEM((n_tile, 4, slots), f32),
            pltpu.VMEM((n_tile, 4, slots), f32),
            [pltpu.VMEM((CHANNELS * PIECES * marks, chunk), jnp.bfloat16)] * 2,
            [pltpu.VMEM((chunk, quarter), jnp.bfloat16)] * 2,
            [pltpu.VMEM((CHANNELS * PIECES * marks, quarter), f32)] * 2,
            pltpu.VMEM((2, CHANNELS, rows, half), f32),
            pltpu.VMEM((CHANNELS, rows, half), f32),
            pltpu.VMEM((CHANNELS, rows, half), f32),
            pltpu.VMEM((CHANNELS, rows, half), f32),
            pltpu.VMEM((rows, half), f32),
            pltpu.VMEM((rows, half), f32),
            pltpu.VMEM((2 * depth, rows, half), f32),
            pltpu.VMEM((2, rows, half), f32),
            pltpu.VMEM((2, rows, LANES), f32),
            pltpu.VMEM((rows, half), f32),
            pltpu.VMEM((rows, half), f32),
            pltpu.VMEM((2, rows, half), f32),
            pltpu.VMEM((rows, half), jnp.int32),
            pltpu.VMEM((2, rows, half), f32),
            pltpu.VMEM((2, rows, half), f32),
            pltpu.VMEM((4, 2, 2, half), f32),
            pltpu.VMEM((4, 2, 2, 2, half), f32),
            pltpu.VMEM((3, 2, rows, LANES), f32),
            pltpu.VMEM((3, 2, 2, rows, LANES), f32),
            pltpu.VMEM((n_tile, 2 * slots), f32),
            pltpu.VMEM((n_tile, slots), f32),
            pltpu.VMEM((n_tile, slots), jnp.int32),
            pltpu.VMEM((1, n_tile), jnp.int32),
            pltpu.SemaphoreType.DMA((11,)),
            pltpu.SemaphoreType.DMA,
            pltpu.SemaphoreType.DMA((groups,)),
            pltpu.SemaphoreType.DMA((2,)),
            pltpu.SemaphoreType.DMA((2,)),
            pltpu.SemaphoreType.DMA((2,)),
            pltpu.SemaphoreType.DMA((4, 2, 2)),
            pltpu.SemaphoreType.DMA((4, 2, 2)),
            pltpu.SemaphoreType.DMA((3, 2)),
            pltpu.SemaphoreType.DMA((3, 2)),
            pltpu.SemaphoreType.DMA((3,)),
            pltpu.SemaphoreType.DMA((3,)),
            pltpu.SemaphoreType.DMA((2,)),
            pltpu.SemaphoreType.DMA((2,)),
        ],
        compiler_params=pltpu.CompilerParams(
            collective_id=0, has_side_effects=True, vmem_limit_bytes=VMEM_BYTES
        ),
    )(
        velocity,
        friction,
        thickness,
        rate,
        driving,
        ice_mask,
        obs_velocity.reshape(n_tile, 2 * slots),
        obs_weight.reshape(n_tile, slots),
        obs_cells.reshape(n_tile, slots),
        obs_counts.reshape(1, n_tile),
    )
    return friction_out, velocity_out


def solution(mesh):
    placed = (
        P(None, "tile", None),
        P("tile", None),
        P("tile", None),
        P("layer", "tile", None),
        P(None, "tile", None),
        P("tile", None),
        P("tile", "layer", None, None),
        P("tile", "layer", None, None),
        P("tile", "layer", None, None),
        P("tile", "layer", None),
    )
    return jax.shard_map(
        body,
        mesh=mesh,
        in_specs=placed,
        out_specs=(P("tile", None), P(None, "tile", None)),
        check_vma=False,
    )
```
